32 devices in a mesh: dp: 16 (over z, x, core), mp: 2 (over y).
Axes of the slice: x: 2, y: 2, z: 4, core: 2. Of those that a mesh axis runs over, the one named last changes fastest.
Arguments:
- inputs: bfloat16 [16384, 768], P('dp'), may hold values from -6 to 6
- segment_ids: int32 [16384], P('dp'), may hold values from 0 to 6, as said below
- pad_flags: int32 [16384], P('dp'), may hold values from 0 to 1, as said below
- w_query: bfloat16 [768, 768], P(None, 'mp'), may hold values from -0.3125 to 0.3125
- w_key: bfloat16 [768, 768], P(None, 'mp'), may hold values from -0.3125 to 0.3125
- w_value: bfloat16 [768, 768], P(None, 'mp'), may hold values from -0.21875 to 0.21875
- b_query: float32 [768], P('mp'), may hold values from -3 to 3
- b_value: float32 [768], P('mp'), may hold values from -3 to 3
- w_proj: bfloat16 [768, 768], P('mp'), may hold values from -0.875 to 0.875
- b_proj: float32 [768], replicated, may hold values from -3 to 3
- gain_attn: float32 [768], replicated, may hold values from 0.5 to 1.5
- shift_attn: float32 [768], replicated, may hold values from -2 to 2
- w_up: bfloat16 [768, 3072], P(None, 'mp'), may hold values from -0.21875 to 0.21875
- b_up: float32 [3072], P('mp'), may hold values from -3 to 3
- w_down: bfloat16 [3072, 768], P('mp'), may hold values from -0.109375 to 0.109375
- b_down: float32 [768], replicated, may hold values from -3 to 3
- gain_ffn: float32 [768], replicated, may hold values from 0.5 to 1.5
- shift_ffn: float32 [768], replicated, may hold values from -2 to 2
- cotangent: bfloat16 [16384, 768], P('dp'), may hold values from -6 to 6
Outputs:
- outputs: bfloat16 [16384, 768], P('dp')
- grad_inputs: float32 [16384, 768], P('dp')
- grad_query: float32 [768, 768], P('dp', 'mp')
- grad_key: float32 [768, 768], P('dp', 'mp')
- grad_value: float32 [768, 768], P('dp', 'mp')
- grad_bquery: float32 [768], P('mp')
- grad_bvalue: float32 [768], P('mp')
- grad_proj: float32 [768, 768], P('mp', 'dp')
- grad_bproj: float32 [768], replicated
- grad_gain_attn: float32 [768], replicated
- grad_shift_attn: float32 [768], replicated
- grad_up: float32 [768, 3072], P('dp', 'mp')
- grad_bup: float32 [3072], P('mp')
- grad_down: float32 [3072, 768], P('mp', 'dp')
- grad_bdown: float32 [768], replicated
- grad_gain_ffn: float32 [768], replicated
- grad_shift_ffn: float32 [768], replicated
The draws below stay inside these ranges and needn't reach their ends.
Inputs may be any that keep to these rules, and one draw needn't show every extreme that they name: `segment_ids`: within each aligned run of 512 tokens (one packed sequence) the ids start at 0 and never fall; the largest, 6, is reached in some sequence of every draw. `pad_flags`: 1 marks padding, which fills the last 1 to 128 tokens of every packed sequence.
All inputs are finite; a program needn't handle non-finite values.
Results may differ from the reference program's by a relative error of at most 0.013.
The reference program's roundings to bfloat16 on the way count: a program that leaves them out, or rounds other values in their place, can miss the bound.
Values sent between devices are 32-bit elements; how exact they have to be, the bound alone decides.
No kernel may reach another device: no remote copies, remote signals or barrier semaphores. Data moves between devices by JAX's collectives and lax.ppermute only.
A program may use at most 192 MiB of HBM per device.

```python
import jax
import jax.numpy as jnp
from jax import lax

D = 768
HEADS = 12
FF = 3072
HD = 64
LENGTH = 512
TOKENS = 16384


def draw_segment_ids(key, part):
    key = jax.random.fold_in(key, 11)
    sequences = TOKENS // LENGTH
    loose_key = jax.random.fold_in(key, 1)
    tight_key = jax.random.fold_in(key, 2)
    choose_key = jax.random.fold_in(key, 3)
    loose_cuts = jax.random.randint(loose_key, (sequences, 6, 1), 1, 2 * LENGTH)
    tight_cuts = jax.random.randint(tight_key, (sequences, 6, 1), 1, LENGTH)
    chosen = jax.random.randint(choose_key, (), 0, sequences)
    which = (jnp.arange(sequences) == chosen)[:, None, None]
    cut_points = jnp.where(which, tight_cuts, loose_cuts)
    positions = jnp.arange(LENGTH)[None, None, :]
    counts = jnp.sum((positions >= cut_points).astype(jnp.int32), axis=1)
    return counts.reshape(TOKENS).astype(jnp.int32)


def draw_pad_flags(key, part):
    key = jax.random.fold_in(key, 23)
    sequences = TOKENS // LENGTH
    pad_len = jax.random.randint(key, (sequences, 1), 1, LENGTH // 4 + 1)
    positions = jnp.arange(LENGTH)[None, :]
    return (positions >= LENGTH - pad_len).astype(jnp.int32).reshape(TOKENS)


def spiked(values, key, source, target, blocks, factor):
    owner, partner = [(jnp.arange(values.shape[axis_at]) // (values.shape[axis_at] // blocks)).reshape([-1 if axis == axis_at else 1 for axis in range(values.ndim)]) for axis_at in (source, target)]
    chosen = jax.random.permutation(key, blocks)[partner]
    strong = (owner == chosen) | (owner == (partner + blocks // 2) % blocks)
    return jnp.where(strong, factor * values, values)


def levels(rng, shape, cuts, smallest, high):
    factor_of = 1.0
    for dim, shards_of in cuts:
        heights = jax.random.uniform(jax.random.fold_in(jax.random.fold_in(rng, 6), dim), (shards_of,), jnp.float32, smallest / len(cuts), high / len(cuts))
        factor_of = factor_of * jnp.repeat(jnp.exp(heights), shape[dim] // shards_of).reshape((-1,) + (1,) * (len(shape) - 1 - dim))
    return factor_of


def noise(rng, shape, deviation, most, cuts=(), kind=jnp.bfloat16):
    level = levels(rng, shape, cuts, -0.22, 0.18) if cuts else 1.0
    drawn = jax.random.normal(rng, shape, jnp.float32) * deviation * level
    return jnp.minimum(jnp.maximum(drawn, -most), most).astype(kind)


def gaussian_with(stream_key, dims, deviation, reach, split, heavy, dtype=jnp.bfloat16):
    entries = deviation * jax.random.normal(stream_key, dims, jnp.float32)
    if split:
        entries = entries * levels(stream_key, dims, split, -0.22, 0.18)
    return jnp.clip(spiked(entries, jax.random.fold_in(stream_key, 3), *heavy), -reach, reach).astype(dtype)


def setup_inputs(seed: int = 0) -> dict:
    key_of = jax.random.split(jax.random.key(seed), 20)
    return {
        "inputs": gaussian_with(key_of[0], (TOKENS, D), 1.0, 6.0, ((0, 16),), (0, 1, 16, 2.0)),
        "segment_ids": draw_segment_ids(jax.random.fold_in(key_of[19], 71), 0),
        "pad_flags": draw_pad_flags(jax.random.fold_in(key_of[19], 71), 0),
        "w_query": noise(key_of[3], (D, D), (D // 2) ** -0.5, 0.3125, ((1, 2),)),
        "w_key": noise(key_of[4], (D, D), (D // 2) ** -0.5, 0.3125, ((1, 2),)),
        "w_value": noise(key_of[5], (D, D), D ** -0.5, 0.21875, ((1, 2),)),
        "b_query": noise(key_of[6], (D,), 0.5, 3.0, ((0, 2),), jnp.float32),
        "b_value": noise(key_of[7], (D,), 0.5, 3.0, ((0, 2),), jnp.float32),
        "w_proj": noise(key_of[8], (D, D), (D // 16) ** -0.5, 0.875, ((0, 2),)),
        "b_proj": noise(key_of[9], (D,), 0.5, 3.0, (), jnp.float32),
        "gain_attn": jnp.clip(1.0 + 0.1 * jax.random.normal(key_of[10], (D,), jnp.float32), 0.5, 1.5),
        "shift_attn": noise(key_of[11], (D,), 0.3, 2.0, (), jnp.float32),
        "w_up": noise(key_of[12], (D, FF), D ** -0.5, 0.21875, ((1, 2),)),
        "b_up": noise(key_of[13], (FF,), 0.5, 3.0, ((0, 2),), jnp.float32),
        "w_down": noise(key_of[14], (FF, D), FF ** -0.5, 0.109375, ((0, 2),)),
        "b_down": noise(key_of[15], (D,), 0.5, 3.0, (), jnp.float32),
        "gain_ffn": jnp.clip(1.0 + 0.1 * jax.random.normal(key_of[16], (D,), jnp.float32), 0.5, 1.5),
        "shift_ffn": noise(key_of[17], (D,), 0.3, 2.0, (), jnp.float32),
        "cotangent": gaussian_with(key_of[18], (TOKENS, D), 1.0, 6.0, ((0, 16),), (0, 1, 16, 2.0)),
    }


@jax.custom_vjp
def low(v):
    return lax.optimization_barrier(v.astype(jnp.bfloat16)).astype(jnp.float32)

@jax.custom_vjp
def low_back(v):
    return v

def low_keep(v):
    return (low(v), None)

def low_pass(kept, grad):
    return (grad,)

def back_keep(v):
    return (v, None)

def back_low(kept, grad):
    return (low(grad),)
low.defvjp(low_keep, low_pass)
low_back.defvjp(back_keep, back_low)
norm_eps = 1e-05
masked_value = -1000000000.0

def matmul(left_mat, right_mat):
    return jnp.dot(left_mat, right_mat, precision=lax.Precision.HIGHEST)

def layer_norm(values, gain_vec, shift_vec):
    average = lax.optimization_barrier(jnp.mean(values, axis=-1, keepdims=True))
    centered = values - average
    variance = lax.optimization_barrier(jnp.mean(centered * centered, axis=-1, keepdims=True))
    return centered * lax.rsqrt(variance + norm_eps) * gain_vec + shift_vec

def gelu_exact(values):
    return 0.5 * values * (1.0 + lax.erf(values * 2.0 ** (-0.5)))

def attend_sequence(pieces):
    queries, key_rows, value_rows, segments, padding = pieces
    head_query = queries.reshape(LENGTH, HEADS, HD)
    head_key = key_rows.reshape(LENGTH, HEADS, HD)
    head_value = value_rows.reshape(LENGTH, HEADS, HD)
    raw_scores = low_back(jnp.einsum('qhd,khd->hqk', head_query, head_key, precision=lax.Precision.HIGHEST))
    scores = raw_scores * HD ** (-0.5)
    positions = jnp.arange(LENGTH)
    allowed = (segments[:, None] == segments[None, :]) & ((padding[None, :] == 0) | (positions[:, None] == positions[None, :]))
    scores = jnp.where(allowed[None], scores, masked_value)
    weights = low(jax.nn.softmax(scores, axis=-1))
    context = jnp.einsum('hqk,khd->qhd', weights, head_value, precision=lax.Precision.HIGHEST)
    return context.reshape(LENGTH, D)

def layer_forward(params, inputs_f, segments, padding):
    w_query, w_key, w_value, b_query, b_value, w_proj, b_proj, gain_attn, shift_attn, w_up, b_up, w_down, b_down, gain_ffn, shift_ffn = params
    queries = low(low_back(matmul(inputs_f, w_query) + b_query))
    key_rows = low(low_back(matmul(inputs_f, w_key)))
    value_rows = low(low_back(matmul(inputs_f, w_value) + b_value))
    sequences = inputs_f.shape[0] // LENGTH

    def shaped(tensor):
        return tensor.reshape((sequences, LENGTH) + tensor.shape[1:])
    context = lax.map(jax.checkpoint(attend_sequence), (shaped(queries), shaped(key_rows), shaped(value_rows), shaped(segments), shaped(padding)))
    context = low(low_back(context.reshape(inputs_f.shape[0], D)))
    attention = low_back(matmul(context, w_proj) + b_proj)
    hidden = inputs_f + attention
    normed = layer_norm(hidden, gain_attn, shift_attn)
    up_value = low_back(matmul(low(normed), w_up) + b_up)
    active = low(gelu_exact(up_value))
    ffn_out = low_back(matmul(active, w_down) + b_down)
    return layer_norm(normed + ffn_out, gain_ffn, shift_ffn)

def reference(inputs, segment_ids, pad_flags, w_query, w_key, w_value, b_query, b_value, w_proj, b_proj, gain_attn, shift_attn, w_up, b_up, w_down, b_down, gain_ffn, shift_ffn, cotangent):
    params = tuple((tensor.astype(jnp.float32) for tensor in (w_query, w_key, w_value, b_query, b_value, w_proj, b_proj, gain_attn, shift_attn, w_up, b_up, w_down, b_down, gain_ffn, shift_ffn)))
    sequences = TOKENS // LENGTH
    group_seqs = 8 if sequences % 8 == 0 else 1
    group_rows = group_seqs * LENGTH
    group_count = TOKENS // group_rows

    def per_group(running, pieces):
        block_in, block_seg, block_pad, block_cot = pieces

        def forward(param_set, values):
            return layer_forward(param_set, values, block_seg, block_pad)
        result, pullback = jax.vjp(forward, params, block_in.astype(jnp.float32))
        grad_params, grad_block = pullback(block_cot.astype(jnp.float32))
        running = tuple((current + addend for current, addend in zip(running, grad_params)))
        return (running, (result.astype(jnp.bfloat16), grad_block))
    zero_grads = tuple((jnp.zeros_like(tensor) for tensor in params))
    running, (outputs, grad_inputs) = lax.scan(per_group, zero_grads, (inputs.reshape(group_count, group_rows, D), segment_ids.reshape(group_count, group_rows), pad_flags.reshape(group_count, group_rows), cotangent.reshape(group_count, group_rows, D)))
    return (outputs.reshape(TOKENS, D), grad_inputs.reshape(TOKENS, D), running[0], running[1], running[2], running[3], running[4], running[5], running[6], running[7], running[8], running[9], running[10], running[11], running[12], running[13], running[14])
```

```python
import functools
import math

import jax
import jax.numpy as jnp
from jax import lax
from jax.experimental import pallas as pl
from jax.experimental.pallas import tpu as pltpu
from jax.sharding import PartitionSpec as P

HD = 64
LENGTH = 512
QUERY_CHUNK = 256
UNIT_BLOCK = 512
norm_eps = 1e-05
masked_value = -1000000000.0
BF = jnp.bfloat16
F32 = jnp.float32
VMEM_BYTES = 50 * 1024 * 1024


def nn(a, b):
    return lax.dot_general(a, b, (((1,), (0,)), ((), ())), preferred_element_type=F32)


def nt(a, b):
    return lax.dot_general(a, b, (((1,), (1,)), ((), ())), preferred_element_type=F32)


def call(body, grid, ins, outs, scratch=(), flops=0):
    def spec(shape, block, index):
        if block == "smem":
            return pl.BlockSpec(memory_space=pltpu.SMEM)
        if block is None:
            return pl.BlockSpec(shape, lambda *_: (0,) * len(shape))
        return pl.BlockSpec(block, index)

    moved = sum(a.size * a.dtype.itemsize for a, _, _ in ins)
    moved += sum(math.prod(s) * jnp.dtype(d).itemsize for s, d, _, _ in outs)
    return pl.pallas_call(
        body,
        grid=grid,
        in_specs=[spec(a.shape, b, i) for a, b, i in ins],
        out_specs=[spec(s, b, i) for s, _, b, i in outs],
        out_shape=[jax.ShapeDtypeStruct(s, d) for s, d, _, _ in outs],
        scratch_shapes=list(scratch),
        compiler_params=pltpu.CompilerParams(vmem_limit_bytes=VMEM_BYTES),
        cost_estimate=pl.CostEstimate(flops=flops, bytes_accessed=moved, transcendentals=0),
    )(*[a for a, _, _ in ins])


def mask_bias(segc_ref, segr_ref, padc_ref, bias_ref):
    shape = bias_ref.shape
    key = lax.broadcasted_iota(jnp.int32, shape, 0)
    query = lax.broadcasted_iota(jnp.int32, shape, 1)
    same = segc_ref[...] == segr_ref[...]
    allowed = same & ((padc_ref[...] == 0) | (key == query))
    bias_ref[...] = jnp.where(allowed, 0.0, masked_value)


def attend_forward(
    x_ref, wq_ref, wk_ref, wv_ref, bq_ref, bv_ref, segc_ref, segr_ref, padc_ref,
    q_ref, k_ref, v_ref, ctx_ref, lse_ref, bias_ref,
):
    x = x_ref[...]
    q_ref[...] = ((nn(x, wq_ref[...]) + bq_ref[...]).astype(BF).astype(F32) * HD ** (-0.5)).astype(BF)
    k_ref[...] = nn(x, wk_ref[...]).astype(BF)
    v_ref[...] = (nn(x, wv_ref[...]) + bv_ref[...]).astype(BF)
    mask_bias(segc_ref, segr_ref, padc_ref, bias_ref)
    length = x.shape[0]

    def pair(index, carry):
        cols = pl.ds(pl.multiple_of(index * 128, 128), 128)
        keys = k_ref[:, cols]
        values_t = v_ref[:, cols].T
        lane = lax.broadcasted_iota(jnp.int32, (QUERY_CHUNK, 128), 1)
        for start in range(0, length, QUERY_CHUNK):
            rows = pl.ds(start, QUERY_CHUNK)
            query = q_ref[rows, cols]
            parts = []
            for head in range(2):
                one = jnp.where((lane < HD) == (head == 0), query, jnp.zeros_like(query))
                scores = nt(keys, one) + bias_ref[:, rows]
                highest = jnp.max(scores, axis=0, keepdims=True)
                grown = jnp.exp(scores - highest)
                total = jnp.sum(grown, axis=0, keepdims=True)
                weights = (grown * (1.0 / total)).astype(BF)
                lse_ref[pl.ds(2 * index + head, 1), rows] = highest + jnp.log(total)
                parts.append(nn(values_t[head * HD:(head + 1) * HD], weights))
            ctx_ref[rows, cols] = jnp.concatenate(parts, axis=0).T.astype(BF)
        return carry

    lax.fori_loop(0, q_ref.shape[1] // 128, pair, 0)


def attend_backward(
    q_ref, k_ref, v_ref, lse_ref, dctx_ref, segc_ref, segr_ref, padc_ref,
    dqkv_ref, sums_ref, bias_ref,
):
    mask_bias(segc_ref, segr_ref, padc_ref, bias_ref)
    length, width = q_ref.shape

    def pair(index, carry):
        first = pl.multiple_of(index * 128, 128)
        cols = pl.ds(first, 128)
        keys = k_ref[:, cols]
        values = v_ref[:, cols]
        keys_t = keys.T
        lane = lax.broadcasted_iota(jnp.int32, (QUERY_CHUNK, 128), 1)
        d_keys = [None, None]
        d_values = [None, None]
        for start in range(0, length, QUERY_CHUNK):
            rows = pl.ds(start, QUERY_CHUNK)
            query = q_ref[rows, cols]
            grad = dctx_ref[rows, cols]
            d_query = []
            for head in range(2):
                here = (lane < HD) == (head == 0)
                scores = nt(keys, jnp.where(here, query, jnp.zeros_like(query))) + bias_ref[:, rows]
                prob = jnp.exp(scores - lse_ref[pl.ds(2 * index + head, 1), rows])
                weights = prob.astype(BF)
                d_prob = nt(values, jnp.where(here, grad, jnp.zeros_like(grad)))
                inner = jnp.sum(prob * d_prob, axis=0, keepdims=True)
                raw = (prob * (d_prob - inner)).astype(BF)
                dv = nn(weights, grad)
                dk = nn(raw, query)
                d_values[head] = dv if start == 0 else d_values[head] + dv
                d_keys[head] = dk if start == 0 else d_keys[head] + dk
                d_query.append(nn(keys_t[head * HD:(head + 1) * HD], raw))
            dq = (jnp.concatenate(d_query, axis=0).T * HD ** (-0.5)).astype(BF)
            dqkv_ref[rows, cols] = dq
        full = lax.broadcasted_iota(jnp.int32, (length, 128), 1) < HD
        dqkv_ref[:, pl.ds(pl.multiple_of(width + first, 128), 128)] = jnp.where(
            full, d_keys[0], d_keys[1]
        ).astype(BF)
        dqkv_ref[:, pl.ds(pl.multiple_of(2 * width + first, 128), 128)] = jnp.where(
            full, d_values[0], d_values[1]
        ).astype(BF)
        return carry

    lax.fori_loop(0, width // 128, pair, 0)
    sums_ref[...] = jnp.broadcast_to(
        jnp.sum(dqkv_ref[...].astype(F32), axis=0, keepdims=True), sums_ref.shape
    )


def moments(values):
    average = jnp.mean(values, axis=-1, keepdims=True)
    centered = values - average
    variance = jnp.mean(centered * centered, axis=-1, keepdims=True)
    inverse = lax.rsqrt(variance + norm_eps)
    return centered * inverse, inverse


def norm_backward(upstream, n, inverse, gain):
    scaled = upstream * gain
    return inverse * (
        scaled
        - jnp.mean(scaled, axis=-1, keepdims=True)
        - n * jnp.mean(scaled * n, axis=-1, keepdims=True)
    )


def down_sum(values):
    return jnp.sum(values, axis=0, keepdims=True)


def feed(nlow, wu_ref, bu_ref, wd_ref, act_ref, slope_ref):
    up = nn(nlow, wu_ref[...]) + bu_ref[...]
    cdf = 0.5 * (1.0 + lax.erf(up * 2.0 ** (-0.5)))
    active = (up * cdf).astype(BF)
    act_ref[...] = active
    slope_ref[...] = cdf + up * jnp.exp(-0.5 * up * up) * (1.0 / math.sqrt(2.0 * math.pi))
    return nn(active, wd_ref[...])


def feed_own(
    x_ref, co_ref, cx_ref, wpo_ref, wpx_ref, bp_ref, g_ref, s_ref, bd_ref, wu_ref, bu_ref, wd_ref,
    hid_ref, nlow_ref, acc_ref, act_ref, slope_ref,
):
    @pl.when(pl.program_id(0) == 0)
    def _():
        attn = nn(co_ref[...], wpo_ref[...]) + nn(cx_ref[...], wpx_ref[...]) + bp_ref[...]
        hidden = x_ref[...].astype(F32) + attn
        hid_ref[...] = hidden
        n, _ = moments(hidden)
        normed = n * g_ref[...] + s_ref[...]
        nlow_ref[...] = normed.astype(BF)
        acc_ref[...] = normed + bd_ref[...]

    acc_ref[...] += feed(nlow_ref[...], wu_ref, bu_ref, wd_ref, act_ref, slope_ref)


def feed_other(
    nlow_ref, start_ref, wu_ref, bu_ref, wd_ref, g_ref, s_ref, cot_ref,
    act_ref, slope_ref, out_ref, dsum_ref, dffn_ref, stats_ref, acc_ref,
):
    @pl.when(pl.program_id(0) == 0)
    def _():
        acc_ref[...] = start_ref[...]

    acc_ref[...] += feed(nlow_ref[...], wu_ref, bu_ref, wd_ref, act_ref, slope_ref)

    @pl.when(pl.program_id(0) == pl.num_programs(0) - 1)
    def _():
        n, inverse = moments(acc_ref[...])
        out_ref[...] = (n * g_ref[...] + s_ref[...]).astype(BF).astype(F32)
        cot = cot_ref[...].astype(F32)
        d_summed = norm_backward(cot, n, inverse, g_ref[...])
        d_ffn = d_summed.astype(BF)
        dsum_ref[...] = d_summed
        dffn_ref[...] = d_ffn
        stats_ref[...] = jnp.zeros_like(stats_ref)
        stats_ref[0:1] = down_sum(cot * n)
        stats_ref[1:2] = down_sum(cot)
        stats_ref[2:3] = down_sum(d_ffn.astype(F32))


def feed_backward(
    dffn_ref, so_ref, sx_ref, wdo_ref, wdx_ref, wuo_ref, wux_ref, dsum_ref, hid_ref, g_ref,
    wpo_ref, wpx_ref,
    duo_ref, dux_ref, bup_ref, dhid_ref, dattn_ref, dco_ref, dcx_ref, stats_ref, acc_ref,
):
    @pl.when(pl.program_id(0) == 0)
    def _():
        acc_ref[...] = dsum_ref[...]

    d_ffn = dffn_ref[...]
    bup_ref[...] = jnp.zeros_like(bup_ref)
    total = acc_ref[...]
    for row, slope, wd, wu, out in (
        (0, so_ref, wdo_ref, wuo_ref, duo_ref),
        (1, sx_ref, wdx_ref, wux_ref, dux_ref),
    ):
        d_up = (nt(d_ffn, wd[...]) * slope[...]).astype(BF)
        out[...] = d_up
        bup_ref[row:row + 1] = down_sum(d_up.astype(F32))
        total += nt(d_up, wu[...])
    acc_ref[...] = total

    @pl.when(pl.program_id(0) == pl.num_programs(0) - 1)
    def _():
        d_normed = acc_ref[...]
        n, inverse = moments(hid_ref[...])
        d_hidden = norm_backward(d_normed, n, inverse, g_ref[...])
        d_attn = d_hidden.astype(BF)
        dhid_ref[...] = d_hidden
        dattn_ref[...] = d_attn
        dco_ref[...] = nt(d_attn, wpo_ref[...]).astype(BF)
        dcx_ref[...] = nt(d_attn, wpx_ref[...]).astype(BF)
        stats_ref[...] = jnp.zeros_like(stats_ref)
        stats_ref[0:1] = down_sum(d_normed * n)
        stats_ref[1:2] = down_sum(d_normed)
        stats_ref[2:3] = down_sum(d_attn.astype(F32))


def input_gradient(*refs):
    dhid_ref, dqo_ref, dqx_ref = refs[:3]
    weights, out_ref = refs[3:9], refs[9]
    total = dhid_ref[...]
    width = weights[0].shape[1]
    for half, grads in enumerate((dqo_ref, dqx_ref)):
        for part in range(3):
            total += nt(grads[:, part * width:(part + 1) * width], weights[half * 3 + part][...])
    out_ref[...] = total


def gradient_split(core_ref, left_ref, own_ref, oth_ref, keep_ref, send_ref, left_t):
    @pl.when(pl.program_id(0) == 0)
    def _():
        left_t[...] = left_ref[...].T

    first = core_ref[0] == 0
    rows = keep_ref.shape[3]
    across = keep_ref.shape[2]
    for half, right in enumerate((own_ref, oth_ref)):
        g = nn(left_t[...], right[...])
        for block in range(keep_ref.shape[1] * across):
            at = 2 * block * rows
            even, odd = g[at:at + rows], g[at + rows:at + 2 * rows]
            keep_ref[half, block // across, block % across] = jnp.where(first, even, odd)
            send_ref[half, block // across, block % across] = jnp.where(first, odd, even)


def gradient_plain(left_ref, own_ref, oth_ref, keep_ref, send_ref, left_t):
    @pl.when(pl.program_id(0) == 0)
    def _():
        left_t[...] = left_ref[...].T

    keep_ref[...] = nn(left_t[...], own_ref[...])
    send_ref[...] = nn(left_t[...], oth_ref[...])


def join_pieces(place_ref, mine_ref, theirs_ref, out_ref):
    same = pl.program_id(0) // 4 == place_ref[0]

    @pl.when(same)
    def _():
        out_ref[...] = mine_ref[0].astype(BF)

    @pl.when(jnp.logical_not(same))
    def _():
        out_ref[...] = theirs_ref[0].astype(BF)


def join_rows(place_ref, mine_ref, theirs_ref, out_ref):
    same = pl.program_id(0) == place_ref[0]

    @pl.when(same)
    def _():
        out_ref[...] = mine_ref[...].astype(out_ref.dtype)

    @pl.when(jnp.logical_not(same))
    def _():
        out_ref[...] = theirs_ref[...].astype(out_ref.dtype)


def both_sequences(place, mine, theirs, dtype):
    rows, cols = mine.shape
    return pl.pallas_call(
        join_rows,
        out_shape=jax.ShapeDtypeStruct((2 * rows, cols), dtype),
        grid_spec=pltpu.PrefetchScalarGridSpec(
            num_scalar_prefetch=1,
            grid=(2,),
            in_specs=[pl.BlockSpec((rows, cols), lambda i, p: (0, 0))] * 2,
            out_specs=pl.BlockSpec((rows, cols), lambda i, p: (i, 0)),
        ),
        compiler_params=pltpu.CompilerParams(vmem_limit_bytes=VMEM_BYTES),
        cost_estimate=pl.CostEstimate(flops=0, bytes_accessed=16 * rows * cols, transcendentals=0),
    )(place, mine, theirs)


def pick(array, index, axis):
    return lax.dynamic_index_in_dim(array, index, axis, keepdims=False)


def on_device(
    dp, inputs, segment_ids, pad_flags, w_query, w_key, w_value, b_query, b_value, w_proj, b_proj,
    gain_attn, shift_attn, w_up, b_up, w_down, b_down, gain_ffn, shift_ffn, cotangent,
):
    m = lax.axis_index("mp")
    d = lax.axis_index("dp")
    width = inputs.shape[1]
    half = w_query.shape[1]
    units = w_up.shape[1]
    core, low = d % 2, (d // 2) % 4

    def swap_mp(array):
        return lax.ppermute(array, "mp", [(0, 1), (1, 0)])

    def swap_dp(array, bit):
        return lax.ppermute(array, "dp", [(i, i ^ bit) for i in range(dp)])

    place_m = jnp.reshape(m, (1,)).astype(jnp.int32)
    place_d = jnp.stack([core, low]).astype(jnp.int32)

    def fetch(pieces):
        own = swap_mp(pieces)
        by_x = swap_dp(own, 2)
        by_z = swap_dp(own, 4)
        cut = own.shape[0] // 2
        far_x = swap_dp(by_z[:cut], 2)
        far_z = swap_dp(by_x[cut:], 4)
        mine = jnp.stack([own, by_x, by_z, jnp.concatenate([far_x, far_z], axis=0)])
        theirs = swap_dp(mine, 1)
        _, rows, cols = mine.shape

        def block(at_mine):
            def index(i, p):
                used = (i // 4 == p[0]) == at_mine
                wait = jnp.where((p[0] == 0) == at_mine, 3, 0)
                return (jnp.bitwise_xor(jnp.where(used, i % 4, wait), p[1]), 0, 0)
            return pl.BlockSpec((1, rows, cols), index)

        return pl.pallas_call(
            join_pieces,
            out_shape=jax.ShapeDtypeStruct((8 * rows, cols), BF),
            grid_spec=pltpu.PrefetchScalarGridSpec(
                num_scalar_prefetch=1,
                grid=(8,),
                in_specs=[block(True), block(False)],
                out_specs=pl.BlockSpec((rows, cols), lambda i, p: (i, 0)),
            ),
            compiler_params=pltpu.CompilerParams(vmem_limit_bytes=VMEM_BYTES),
            cost_estimate=pl.CostEstimate(
                flops=0, bytes_accessed=48 * rows * cols, transcendentals=0
            ),
        )(place_d, mine, theirs)

    def eighth(weight):
        rows = weight.shape[0] // 8
        return lax.dynamic_slice_in_dim(weight, (core * 4 + low) * rows, rows, 0).astype(F32)

    qkv_oth = fetch(jnp.concatenate([eighth(w_query), eighth(w_key), eighth(w_value)], axis=1))
    proj_oth = fetch(eighth(w_proj))
    up_oth = fetch(eighth(w_up))
    down_oth = fetch(eighth(w_down))
    bias_oth = swap_mp(jnp.concatenate([b_query, b_value, b_up]).reshape(1, -1))
    bq_oth, bv_oth, bu_oth = (
        bias_oth[:, :half], bias_oth[:, half:2 * half], bias_oth[:, 2 * half:],
    )

    def row(vector):
        return vector.reshape(1, -1)

    own = lambda array: lax.dynamic_slice_in_dim(array, m * LENGTH, LENGTH, 0)
    x, cot = own(inputs), own(cotangent)
    seg, pad = own(segment_ids), own(pad_flags)
    masks = [(seg.reshape(-1, 1), None, None), (row(seg), None, None), (pad.reshape(-1, 1), None, None)]
    square = pltpu.VMEM((LENGTH, LENGTH), F32)
    heads = half // HD
    lanes = (LENGTH, half)

    def attend(weights, bq, bv):
        return call(
            attend_forward, (1,),
            [(x, None, None)] + weights + [(bq, None, None), (bv, None, None)] + masks,
            [(lanes, BF, None, None)] * 4 + [((heads, LENGTH), F32, None, None)],
            [square], flops=6 * LENGTH * width * half + 16 * LENGTH * LENGTH * half,
        )

    def column(array, at):
        return (array, (array.shape[0], half), lambda *_: (0, at))

    own_qkv = [(w_query, None, None), (w_key, None, None), (w_value, None, None)]
    oth_qkv = [column(qkv_oth, at) for at in range(3)]
    q_own, k_own, v_own, ctx_own, lse_own = attend(own_qkv, row(b_query), row(b_value))
    q_oth, k_oth, v_oth, ctx_oth, lse_oth = attend(oth_qkv, bq_oth, bv_oth)

    full = lambda array: (array, None, None)
    steps = units // UNIT_BLOCK
    feed_ins = lambda wu, bu, wd: [
        (wu, (width, UNIT_BLOCK), lambda i: (0, i)),
        (bu, (1, UNIT_BLOCK), lambda i: (0, i)),
        (wd, (UNIT_BLOCK, width), lambda i: (i, 0)),
    ]
    unit_cols = lambda dtype: ((LENGTH, units), dtype, (LENGTH, UNIT_BLOCK), lambda i: (0, i))
    token = lambda dtype: ((LENGTH, width), dtype, None, None)
    stat = ((8, width), F32, None, None)
    hidden, normed_low, partial, act_own, slope_own = call(
        feed_own, (steps,),
        [full(x), full(ctx_own), full(ctx_oth), full(w_proj), full(proj_oth), full(row(b_proj)),
         full(row(gain_attn)), full(row(shift_attn)), full(row(b_down))]
        + feed_ins(w_up, row(b_up), w_down),
        [token(F32), token(BF), token(F32), unit_cols(BF), unit_cols(F32)],
        flops=4 * LENGTH * width * (half + units),
    )
    act_oth, slope_oth, out_own, d_summed, d_ffn, stats_ffn = call(
        feed_other, (steps,),
        [full(normed_low), full(partial)] + feed_ins(up_oth, bu_oth, down_oth)
        + [full(row(gain_ffn)), full(row(shift_ffn)), full(cot)],
        [unit_cols(BF), unit_cols(F32), token(F32), token(F32), token(BF), stat],
        [pltpu.VMEM((LENGTH, width), F32)],
        flops=4 * LENGTH * width * units,
    )
    out_theirs = swap_mp(out_own)

    shards = dp if dp == 16 else 0
    core_arg = jnp.reshape(core, (1,)).astype(jnp.int32)

    def gradient(left, right_own, right_oth, block, start=0, count=None):
        count = count or right_own.shape[1] // block
        cols = count * block
        ins = [
            full(left),
            (right_own, (LENGTH, block), lambda i: (0, i + start)),
            (right_oth, (LENGTH, block), lambda i: (0, i + start)),
        ]
        scratch = [pltpu.VMEM((width, LENGTH), BF)]
        flops = 4 * LENGTH * width * cols
        if not shards:
            plain = ((width, cols), F32, (width, block), lambda i: (0, i))
            return call(gradient_plain, (count,), ins, [plain] * 2, scratch, flops)
        lead = (2, dp // 4, 2, width // dp)
        cut = (lead + (cols,), F32, lead + (block,), lambda i: (0, 0, 0, 0, i))
        return call(
            gradient_split, (count,), [(core_arg, "smem", None)] + ins, [cut] * 2, scratch, flops
        )

    cross, along = (d // 2) % 2, d // 4
    length_z = dp // 4

    def over_y(v):
        return pick(v, 0, 0) + swap_mp(pick(v, 1, 0))

    def over_x(v, axis):
        return pick(v, cross, axis) + swap_dp(pick(v, 1 - cross, axis), 2)

    def over_z(v, axis):
        shard = lambda at: pick(v, jnp.clip(at, 0, length_z - 1), axis)
        right = left = None
        for step in range(1, length_z):
            ahead, behind = shard(along + length_z - step), shard(along - length_z + step)
            if right is not None:
                ahead, behind = ahead + right, behind + left
            right = lax.ppermute(
                ahead, "dp", [(i, i + 4) for i in range(dp) if i // 4 < step]
            )
            left = lax.ppermute(
                behind, "dp", [(i, i - 4) for i in range(dp) if i // 4 >= length_z - step]
            )
        return shard(along) + right + left

    def reduce(keep, send, order):
        if not shards:
            total = keep + swap_mp(send)
            return lax.psum_scatter(total, "dp", scatter_dimension=0, tiled=True)
        v = keep + swap_dp(send, 1)
        names = ["h", "z", "x"]
        for stage in order:
            axis = names.index({"y": "h"}.get(stage, stage))
            if stage == "y":
                v = over_y(v)
            elif stage == "x":
                v = over_x(v, axis)
            else:
                v = over_z(v, axis)
            names.pop(axis)
        return v

    def everyone(vector):
        if not shards:
            return lax.psum(vector, "dp")
        for bit in (1, 2, 4, 8):
            vector = vector + swap_dp(vector, bit)
        return vector

    chunk = units // 2 // 384
    down_parts = [
        reduce(*gradient(d_ffn, act_own, act_oth, 384, at * chunk, chunk), "xzy") for at in range(2)
    ]
    tokens_by_units = lambda array: (array, (LENGTH, UNIT_BLOCK), lambda i: (0, i))
    down_block = lambda array: (array, (UNIT_BLOCK, width), lambda i: (i, 0))
    up_block = lambda array: (array, (width, UNIT_BLOCK), lambda i: (0, i))
    dup_own, dup_oth, sums_up, d_hidden, d_attn, dctx_own, dctx_oth, stats_attn = call(
        feed_backward, (steps,),
        [full(d_ffn), tokens_by_units(slope_own), tokens_by_units(slope_oth), down_block(w_down),
         down_block(down_oth), up_block(w_up), up_block(up_oth), full(d_summed), full(hidden),
         full(row(gain_attn)), full(w_proj), full(proj_oth)],
        [unit_cols(BF), unit_cols(BF), ((8, units), F32, (8, UNIT_BLOCK), lambda i: (0, i)),
         token(F32), token(BF), (lanes, BF, None, None), (lanes, BF, None, None), stat],
        [pltpu.VMEM((LENGTH, width), F32)],
        flops=8 * LENGTH * width * units,
    )
    up_parts = [
        reduce(*gradient(normed_low, dup_own, dup_oth, 384, at * chunk, chunk), "yxz")
        for at in range(2)
    ]
    common = jnp.concatenate([stats_ffn[:3], stats_attn[:3]], axis=0)
    early = jnp.concatenate([common, sums_up[0].reshape(-1, width)], axis=0) + swap_mp(
        jnp.concatenate([common, sums_up[1].reshape(-1, width)], axis=0)
    )
    early = everyone(early)

    proj_part = reduce(*gradient(d_attn, ctx_own, ctx_oth, half), "xzy")

    def attend_back(q, k, v, lse, dctx):
        return call(
            attend_backward, (1,),
            [full(q), full(k), full(v), full(lse), full(dctx)] + masks,
            [((LENGTH, 3 * half), BF, None, None), ((8, 3 * half), F32, None, None)],
            [square], flops=40 * LENGTH * LENGTH * half,
        )

    dqkv_own, sums_own = attend_back(q_own, k_own, v_own, lse_own, dctx_own)
    dqkv_oth, sums_oth = attend_back(q_oth, k_oth, v_oth, lse_oth, dctx_oth)
    (grad_x,) = call(
        input_gradient, (1,),
        [full(d_hidden), full(dqkv_own), full(dqkv_oth)] + own_qkv + oth_qkv,
        [token(F32)], flops=12 * LENGTH * width * half,
    )
    grad_x_theirs = swap_mp(grad_x)
    qkv_part = reduce(*gradient(x, dqkv_own, dqkv_oth, half), "zxy")

    def ends(sums):
        return jnp.concatenate([sums[:1, :half], sums[:1, 2 * half:]], axis=1)

    late = everyone(ends(sums_own) + swap_mp(ends(sums_oth)))

    outputs = both_sequences(place_m, out_own, out_theirs, BF)
    grad_inputs = both_sequences(place_m, grad_x, grad_x_theirs, F32)
    grad_up = jnp.concatenate(up_parts, axis=1)
    grad_down = jnp.concatenate(down_parts, axis=1).T
    return (
        outputs,
        grad_inputs,
        qkv_part[:, :half],
        qkv_part[:, half:2 * half],
        qkv_part[:, 2 * half:],
        late[0, :half],
        late[0, half:],
        proj_part.T,
        early[5],
        early[3],
        early[4],
        grad_up,
        early[6:].reshape(-1),
        grad_down,
        early[2],
        early[0],
        early[1],
    )


def solution(mesh):
    placed = (
        P("dp", None), P("dp"), P("dp"), P(None, "mp"), P(None, "mp"), P(None, "mp"), P("mp"),
        P("mp"), P("mp", None), P(), P(), P(), P(None, "mp"), P("mp"), P("mp", None), P(), P(), P(),
        P("dp", None),
    )
    return jax.shard_map(
        functools.partial(on_device, mesh.shape["dp"]),
        mesh=mesh,
        in_specs=placed,
        out_specs=(
            P("dp", None), P("dp", None), P("dp", "mp"), P("dp", "mp"), P("dp", "mp"), P("mp"),
            P("mp"), P("mp", "dp"), P(), P(), P(), P("dp", "mp"), P("mp"), P("mp", "dp"), P(), P(),
            P(),
        ),
        check_vma=False,
    )
```

```python
import functools
import math

import jax
import jax.numpy as jnp
from jax import lax
from jax.experimental import pallas as pl
from jax.experimental.pallas import tpu as pltpu
from jax.sharding import PartitionSpec as P

HD = 64
LENGTH = 512
QUERY_CHUNK = 256
UNIT_BLOCK = 512
norm_eps = 1e-05
masked_value = -1000000000.0
BF = jnp.bfloat16
F32 = jnp.float32
VMEM_BYTES = 50 * 1024 * 1024


def nn(a, b):
    return lax.dot_general(a, b, (((1,), (0,)), ((), ())), preferred_element_type=F32)


def nt(a, b):
    return lax.dot_general(a, b, (((1,), (1,)), ((), ())), preferred_element_type=F32)


def call(body, grid, ins, outs, scratch=(), micros=1.0):
    def spec(shape, block, index):
        if block == "smem":
            return pl.BlockSpec(memory_space=pltpu.SMEM)
        if block is None:
            return pl.BlockSpec(shape, lambda *_: (0,) * len(shape))
        return pl.BlockSpec(block, index)

    moved = sum(a.size * a.dtype.itemsize for a, _, _ in ins)
    moved += sum(math.prod(s) * jnp.dtype(d).itemsize for s, d, _, _ in outs)
    return pl.pallas_call(
        body,
        grid=grid,
        in_specs=[spec(a.shape, b, i) for a, b, i in ins],
        out_specs=[spec(s, b, i) for s, _, b, i in outs],
        out_shape=[jax.ShapeDtypeStruct(s, d) for s, d, _, _ in outs],
        scratch_shapes=list(scratch),
        compiler_params=pltpu.CompilerParams(vmem_limit_bytes=VMEM_BYTES),
        cost_estimate=pl.CostEstimate(
            flops=int(micros * 1.15e9), bytes_accessed=moved, transcendentals=0
        ),
    )(*[a for a, _, _ in ins])


def mask_bias(segc_ref, segr_ref, padc_ref, bias_ref):
    shape = bias_ref.shape
    key = lax.broadcasted_iota(jnp.int32, shape, 0)
    query = lax.broadcasted_iota(jnp.int32, shape, 1)
    same = segc_ref[...] == segr_ref[...]
    allowed = same & ((padc_ref[...] == 0) | (key == query))
    bias_ref[...] = jnp.where(allowed, 0.0, masked_value)


def attend_forward(
    x_ref, wq_ref, wk_ref, wv_ref, bq_ref, bv_ref, segc_ref, segr_ref, padc_ref,
    q_ref, k_ref, v_ref, ctx_ref, lse_ref, bias_ref,
):
    x = x_ref[...]
    q_ref[...] = ((nn(x, wq_ref[...]) + bq_ref[...]).astype(BF).astype(F32) * HD ** (-0.5)).astype(BF)
    k_ref[...] = nn(x, wk_ref[...]).astype(BF)
    v_ref[...] = (nn(x, wv_ref[...]) + bv_ref[...]).astype(BF)
    mask_bias(segc_ref, segr_ref, padc_ref, bias_ref)
    length = x.shape[0]

    def pair(index, carry):
        cols = pl.ds(pl.multiple_of(index * 128, 128), 128)
        keys = k_ref[:, cols]
        values_t = v_ref[:, cols].T
        lane = lax.broadcasted_iota(jnp.int32, (QUERY_CHUNK, 128), 1)
        for start in range(0, length, QUERY_CHUNK):
            rows = pl.ds(start, QUERY_CHUNK)
            query = q_ref[rows, cols]
            parts = []
            for head in range(2):
                one = jnp.where((lane < HD) == (head == 0), query, jnp.zeros_like(query))
                scores = nt(keys, one) + bias_ref[:, rows]
                highest = jnp.max(scores, axis=0, keepdims=True)
                grown = jnp.exp(scores - highest)
                total = jnp.sum(grown, axis=0, keepdims=True)
                weights = (grown * (1.0 / total)).astype(BF)
                lse_ref[pl.ds(2 * index + head, 1), rows] = highest + jnp.log(total)
                parts.append(nn(values_t[head * HD:(head + 1) * HD], weights))
            ctx_ref[rows, cols] = jnp.concatenate(parts, axis=0).T.astype(BF)
        return carry

    lax.fori_loop(0, q_ref.shape[1] // 128, pair, 0)


def attend_backward(
    q_ref, k_ref, v_ref, lse_ref, dctx_ref, segc_ref, segr_ref, padc_ref,
    dqkv_ref, sums_ref, bias_ref,
):
    mask_bias(segc_ref, segr_ref, padc_ref, bias_ref)
    length, width = q_ref.shape

    def pair(index, carry):
        first = pl.multiple_of(index * 128, 128)
        cols = pl.ds(first, 128)
        keys = k_ref[:, cols]
        values = v_ref[:, cols]
        keys_t = keys.T
        lane = lax.broadcasted_iota(jnp.int32, (QUERY_CHUNK, 128), 1)
        d_keys = [None, None]
        d_values = [None, None]
        for start in range(0, length, QUERY_CHUNK):
            rows = pl.ds(start, QUERY_CHUNK)
            query = q_ref[rows, cols]
            grad = dctx_ref[rows, cols]
            d_query = []
            for head in range(2):
                here = (lane < HD) == (head == 0)
                scores = nt(keys, jnp.where(here, query, jnp.zeros_like(query))) + bias_ref[:, rows]
                prob = jnp.exp(scores - lse_ref[pl.ds(2 * index + head, 1), rows])
                weights = prob.astype(BF)
                d_prob = nt(values, jnp.where(here, grad, jnp.zeros_like(grad)))
                inner = jnp.sum(prob * d_prob, axis=0, keepdims=True)
                raw = (prob * (d_prob - inner)).astype(BF)
                dv = nn(weights, grad)
                dk = nn(raw, query)
                d_values[head] = dv if start == 0 else d_values[head] + dv
                d_keys[head] = dk if start == 0 else d_keys[head] + dk
                d_query.append(nn(keys_t[head * HD:(head + 1) * HD], raw))
            dq = (jnp.concatenate(d_query, axis=0).T * HD ** (-0.5)).astype(BF)
            dqkv_ref[rows, cols] = dq
        full = lax.broadcasted_iota(jnp.int32, (length, 128), 1) < HD
        dqkv_ref[:, pl.ds(pl.multiple_of(width + first, 128), 128)] = jnp.where(
            full, d_keys[0], d_keys[1]
        ).astype(BF)
        dqkv_ref[:, pl.ds(pl.multiple_of(2 * width + first, 128), 128)] = jnp.where(
            full, d_values[0], d_values[1]
        ).astype(BF)
        return carry

    lax.fori_loop(0, width // 128, pair, 0)
    sums_ref[...] = jnp.broadcast_to(
        jnp.sum(dqkv_ref[...].astype(F32), axis=0, keepdims=True), sums_ref.shape
    )


def moments(values):
    average = jnp.mean(values, axis=-1, keepdims=True)
    centered = values - average
    variance = jnp.mean(centered * centered, axis=-1, keepdims=True)
    inverse = lax.rsqrt(variance + norm_eps)
    return centered * inverse, inverse


def norm_backward(upstream, n, inverse, gain):
    scaled = upstream * gain
    return inverse * (
        scaled
        - jnp.mean(scaled, axis=-1, keepdims=True)
        - n * jnp.mean(scaled * n, axis=-1, keepdims=True)
    )


def down_sum(values):
    return jnp.sum(values, axis=0, keepdims=True)


def activate(nlow, wu_ref, bu_ref, act_ref=None, slope_ref=None):
    up = nn(nlow, wu_ref[...]) + bu_ref[...]
    cdf = 0.5 * (1.0 + lax.erf(up * 2.0 ** (-0.5)))
    active = (up * cdf).astype(BF)
    if act_ref is not None:
        act_ref[...] = active
        slope_ref[...] = cdf + up * jnp.exp(-0.5 * up * up) * (1.0 / math.sqrt(2.0 * math.pi))
    return active


def feed_own(
    x_ref, co_ref, cx_ref, wpo_ref, wpx_ref, bp_ref, g_ref, s_ref, bd_ref, wu_ref, bu_ref, wd_ref,
    hid_ref, normed_ref, nlow_ref, acc_ref, act_ref, slope_ref,
):
    @pl.when(pl.program_id(0) == 0)
    def _():
        attn = nn(co_ref[...], wpo_ref[...]) + nt(cx_ref[...], wpx_ref[...]) + bp_ref[...]
        hidden = x_ref[...].astype(F32) + attn
        hid_ref[...] = hidden
        n, _ = moments(hidden)
        normed = n * g_ref[...] + s_ref[...]
        normed_ref[...] = normed
        nlow_ref[...] = normed.astype(BF)
        acc_ref[...] = normed + bd_ref[...]

    acc_ref[...] += nn(activate(nlow_ref[...], wu_ref, bu_ref, act_ref, slope_ref), wd_ref[...])


def second_norm(total, g_ref, s_ref, cot_ref, out_ref, dffn_ref):
    n, inverse = moments(total)
    out_ref[...] = (n * g_ref[...] + s_ref[...]).astype(BF)
    cot = cot_ref[...].astype(F32)
    d_summed = norm_backward(cot, n, inverse, g_ref[...])
    dffn_ref[...] = d_summed.astype(BF)
    return n, cot, d_summed


def feed_other(
    nlow_ref, start_ref, wu_ref, bu_ref, wd_ref, g_ref, s_ref, cot_ref,
    act_ref, slope_ref, out_ref, dsum_ref, dffn_ref, stats_ref, acc_ref,
):
    @pl.when(pl.program_id(0) == 0)
    def _():
        acc_ref[...] = start_ref[...]

    acc_ref[...] += nt(activate(nlow_ref[...], wu_ref, bu_ref, act_ref, slope_ref), wd_ref[...])

    @pl.when(pl.program_id(0) == pl.num_programs(0) - 1)
    def _():
        n, cot, d_summed = second_norm(acc_ref[...], g_ref, s_ref, cot_ref, out_ref, dffn_ref)
        dsum_ref[...] = d_summed
        stats_ref[...] = jnp.zeros_like(stats_ref)
        stats_ref[0:1] = down_sum(cot * n)
        stats_ref[1:2] = down_sum(cot)
        stats_ref[2:3] = down_sum(d_summed.astype(BF).astype(F32))


def feed_partner(
    normed_ref, wuo_ref, buo_ref, wdo_ref, wux_ref, bux_ref, wdx_ref, g_ref, s_ref, bd_ref, cot_ref,
    nlow_ref, act_ref, slope_ref, out_ref, dffn_ref, acc_ref,
):
    @pl.when(pl.program_id(0) == 0)
    def _():
        nlow_ref[...] = normed_ref[...].astype(BF)
        acc_ref[...] = normed_ref[...] + bd_ref[...]

    nlow = nlow_ref[...]
    acc_ref[...] += nn(activate(nlow, wuo_ref, buo_ref, act_ref, slope_ref), wdo_ref[...])
    acc_ref[...] += nt(activate(nlow, wux_ref, bux_ref), wdx_ref[...])

    @pl.when(pl.program_id(0) == pl.num_programs(0) - 1)
    def _():
        second_norm(acc_ref[...], g_ref, s_ref, cot_ref, out_ref, dffn_ref)


def feed_backward(
    dffn_ref, dffnp_ref, so_ref, sx_ref, sp_ref, wdo_ref, wdx_ref, wuo_ref, wux_ref, dsum_ref,
    hid_ref, g_ref, wpo_ref, wpx_ref,
    duo_ref, dup_ref, bup_ref, dhid_ref, dattn_ref, dco_ref, dcx_ref, stats_ref, acc_ref,
):
    @pl.when(pl.program_id(0) == 0)
    def _():
        acc_ref[...] = dsum_ref[...]

    d_ffn = dffn_ref[...]
    d_own = (nt(d_ffn, wdo_ref[...]) * so_ref[...]).astype(BF)
    d_partner = (nt(dffnp_ref[...], wdo_ref[...]) * sp_ref[...]).astype(BF)
    d_other = (nn(d_ffn, wdx_ref[...]) * sx_ref[...]).astype(BF)
    duo_ref[...] = d_own
    dup_ref[...] = d_partner
    bup_ref[...] = jnp.broadcast_to(
        down_sum(d_own.astype(F32)) + down_sum(d_partner.astype(F32)), bup_ref.shape
    )
    acc_ref[...] += nt(d_own, wuo_ref[...]) + nt(d_other, wux_ref[...])

    @pl.when(pl.program_id(0) == pl.num_programs(0) - 1)
    def _():
        d_normed = acc_ref[...]
        n, inverse = moments(hid_ref[...])
        d_hidden = norm_backward(d_normed, n, inverse, g_ref[...])
        d_attn = d_hidden.astype(BF)
        dhid_ref[...] = d_hidden
        dattn_ref[...] = d_attn
        dco_ref[...] = nt(d_attn, wpo_ref[...]).astype(BF)
        dcx_ref[...] = nn(d_attn, wpx_ref[...]).astype(BF)
        stats_ref[...] = jnp.zeros_like(stats_ref)
        stats_ref[0:1] = down_sum(d_normed * n)
        stats_ref[1:2] = down_sum(d_normed)
        stats_ref[2:3] = down_sum(d_attn.astype(F32))


def input_gradient(*refs):
    dhid_ref, dqo_ref, dqx_ref = refs[:3]
    weights, out_ref = refs[3:9], refs[9]
    total = dhid_ref[...]
    width = weights[0].shape[1]
    for half, grads in enumerate((dqo_ref, dqx_ref)):
        for part in range(3):
            total += nt(grads[:, part * width:(part + 1) * width], weights[half * 3 + part][...])
    out_ref[...] = total


def scatter_rows(g, first, keep_ref, send_ref, lead):
    _, over, across, rows = keep_ref.shape[-5:-1]
    for block in range(keep_ref.shape[-5] * over * across):
        at = 2 * block * rows
        even, odd = g[at:at + rows], g[at + rows:at + 2 * rows]
        place = lead + (block // (over * across), block // across % over, block % across)
        keep_ref[place] = jnp.where(first, even, odd)
        send_ref[place] = jnp.where(first, odd, even)


def gradient_halves(core_ref, left_ref, own_ref, oth_ref, keep_ref, send_ref, left_t):
    @pl.when(pl.program_id(0) == 0)
    def _():
        left_t[...] = left_ref[...].T

    first = core_ref[0] == 0
    for half, right in enumerate((own_ref, oth_ref)):
        scatter_rows(nn(left_t[...], right[...]), first, keep_ref, send_ref, (half,))


def gradient_tokens(core_ref, la_ref, lb_ref, ra_ref, rb_ref, keep_ref, send_ref, a_t, b_t):
    @pl.when(pl.program_id(0) == 0)
    def _():
        a_t[...] = la_ref[...].T
        b_t[...] = lb_ref[...].T

    g = nn(a_t[...], ra_ref[...]) + nn(b_t[...], rb_ref[...])
    scatter_rows(g, core_ref[0] == 0, keep_ref, send_ref, ())


def plain_halves(left_ref, own_ref, oth_ref, keep_ref, send_ref, left_t):
    @pl.when(pl.program_id(0) == 0)
    def _():
        left_t[...] = left_ref[...].T

    keep_ref[...] = nn(left_t[...], own_ref[...])
    send_ref[...] = nn(left_t[...], oth_ref[...])


def plain_tokens(la_ref, lb_ref, ra_ref, rb_ref, out_ref, a_t, b_t):
    @pl.when(pl.program_id(0) == 0)
    def _():
        a_t[...] = la_ref[...].T
        b_t[...] = lb_ref[...].T

    out_ref[...] = nn(a_t[...], ra_ref[...]) + nn(b_t[...], rb_ref[...])


def join_pieces(place_ref, near_ref, far_ref, near_core_ref, far_core_ref, out_ref):
    rows = far_ref.shape[0]
    for mine, near, far in ((True, near_ref, far_ref), (False, near_core_ref, far_core_ref)):
        base = (place_ref[0] if mine else 1 - place_ref[0]) * 4
        for piece in range(4):
            at = (base + jnp.bitwise_xor(place_ref[1], piece)) * rows
            value = far[...] if piece == 3 else near[piece]
            out_ref[pl.ds(pl.multiple_of(at, 16), rows)] = value.astype(BF)


def join_rows(place_ref, mine_ref, theirs_ref, out_ref):
    same = pl.program_id(0) == place_ref[0]

    @pl.when(same)
    def _():
        out_ref[...] = mine_ref[...].astype(out_ref.dtype)

    @pl.when(jnp.logical_not(same))
    def _():
        out_ref[...] = theirs_ref[...].astype(out_ref.dtype)


def both_sequences(place, mine, theirs, dtype):
    rows, cols = mine.shape
    return pl.pallas_call(
        join_rows,
        out_shape=jax.ShapeDtypeStruct((2 * rows, cols), dtype),
        grid_spec=pltpu.PrefetchScalarGridSpec(
            num_scalar_prefetch=1,
            grid=(2,),
            in_specs=[pl.BlockSpec((rows, cols), lambda i, p: (0, 0))] * 2,
            out_specs=pl.BlockSpec((rows, cols), lambda i, p: (i, 0)),
        ),
        compiler_params=pltpu.CompilerParams(vmem_limit_bytes=VMEM_BYTES),
        cost_estimate=pl.CostEstimate(flops=0, bytes_accessed=16 * rows * cols, transcendentals=0),
    )(place, mine, theirs)


def pick(array, index, axis):
    return lax.dynamic_index_in_dim(array, index, axis, keepdims=False)


def on_device(
    dp, inputs, segment_ids, pad_flags, w_query, w_key, w_value, b_query, b_value, w_proj, b_proj,
    gain_attn, shift_attn, w_up, b_up, w_down, b_down, gain_ffn, shift_ffn, cotangent,
):
    m = lax.axis_index("mp")
    d = lax.axis_index("dp")
    width = inputs.shape[1]
    half = w_query.shape[1]
    units = w_up.shape[1]
    core, low = d % 2, (d // 2) % 4

    def swap_mp(array):
        return lax.ppermute(array, "mp", [(0, 1), (1, 0)])

    def swap_dp(array, bit):
        return lax.ppermute(array, "dp", [(i, i ^ bit) for i in range(dp)])

    place_m = jnp.reshape(m, (1,)).astype(jnp.int32)
    place_d = jnp.stack([core, low]).astype(jnp.int32)

    rows = width // 8

    def eighth(weight):
        return lax.dynamic_slice_in_dim(weight, (core * 4 + low) * rows, rows, 0).astype(F32)

    def eighth_t(weight):
        return lax.dynamic_slice_in_dim(weight, (core * 4 + low) * rows, rows, 1).T.astype(F32)

    def after(arrays, *others):
        return lax.optimization_barrier((tuple(arrays), others))[0]

    def near_pieces(own):
        return swap_dp(own, 2), swap_dp(own, 4)

    def far_pieces(by_x, by_z):
        return swap_dp(by_z[:rows // 2], 2), swap_dp(by_x[rows // 2:], 4)

    def join(own, by_x, by_z, far_x, far_z):
        near = jnp.stack([own, by_x, by_z])
        far = jnp.concatenate([far_x, far_z], axis=0)
        near_core, far_core = swap_dp(near, 1), swap_dp(far, 1)
        (joined,) = call(
            join_pieces, (1,),
            [(place_d, "smem", None)]
            + [(a, None, None) for a in (near, far, near_core, far_core)],
            [((width, own.shape[1]), BF, None, None)],
            micros=3.0,
        )
        return joined

    def row(vector):
        return vector.reshape(1, -1)

    own = lambda array: lax.dynamic_slice_in_dim(array, m * LENGTH, LENGTH, 0)
    x, cot = own(inputs), own(cotangent)
    cot_partner = lax.dynamic_slice_in_dim(cotangent, (1 - m) * LENGTH, LENGTH, 0)
    seg, pad = own(segment_ids), own(pad_flags)
    masks = [(seg.reshape(-1, 1), None, None), (row(seg), None, None), (pad.reshape(-1, 1), None, None)]
    square = pltpu.VMEM((LENGTH, LENGTH), F32)
    heads = half // HD
    lanes = (LENGTH, half)

    def attend(weights, bq, bv):
        return call(
            attend_forward, (1,),
            [(x, None, None)] + weights + [(bq, None, None), (bv, None, None)] + masks,
            [(lanes, BF, None, None)] * 4 + [((heads, LENGTH), F32, None, None)],
            [square], micros=9.0,
        )

    def column(array, at):
        return (array, (array.shape[0], half), lambda *_: (0, at))

    full = lambda array: (array, None, None)
    extra = jnp.concatenate([b_query, b_value, b_up])
    extra = jnp.pad(extra, (0, 8 * units - extra.size)).reshape(8, units)
    first = jnp.concatenate(
        [eighth(w_query), eighth(w_key), eighth(w_value), eighth_t(w_proj)], axis=1
    )
    first = swap_mp(jnp.concatenate([first, extra], axis=0))
    extra = first[rows:].reshape(1, -1)
    first = first[:rows]
    bq_oth, bv_oth, bu_oth = (
        extra[:, :half], extra[:, half:2 * half], extra[:, 2 * half:2 * half + units],
    )
    own_qkv = [full(w_query), full(w_key), full(w_value)]
    q_own, k_own, v_own, ctx_own, lse_own = attend(own_qkv, row(b_query), row(b_value))
    first, send_second = after((first, eighth(w_up)), ctx_own)
    second = swap_mp(send_second)
    first_x, first_z = near_pieces(first)
    (second,) = after((second,), first_x, first_z)
    first_far = far_pieces(first_x, first_z)
    third = swap_mp(after((eighth_t(w_down),), second)[0])
    joined = join(first, first_x, first_z, *first_far)
    (second,) = after((second,), *first_far)
    second_x, second_z = near_pieces(second)
    oth_qkv = [column(joined, at) for at in range(3)]
    proj_oth = column(joined, 3)
    q_oth, k_oth, v_oth, ctx_oth, lse_oth = attend(oth_qkv, bq_oth, bv_oth)
    second_x, second_z, third = after((second_x, second_z, third), ctx_oth)
    second_far = far_pieces(second_x, second_z)
    (third,) = after((third,), second_x, second_z)
    third_x, third_z = near_pieces(third)

    steps = units // UNIT_BLOCK
    unit_row = lambda array: (array, (1, UNIT_BLOCK), lambda i: (0, i))
    unit_col = lambda array: (array, (array.shape[0], UNIT_BLOCK), lambda i: (0, i))
    unit_block = lambda array: (array, (UNIT_BLOCK, width), lambda i: (i, 0))
    unit_out = lambda dtype: ((LENGTH, units), dtype, (LENGTH, UNIT_BLOCK), lambda i: (0, i))
    token = lambda dtype: ((LENGTH, width), dtype, None, None)
    stat = ((8, width), F32, None, None)
    total = pltpu.VMEM((LENGTH, width), F32)
    own_up = [unit_col(w_up), unit_row(row(b_up)), unit_block(w_down)]
    ffn_norm = [full(row(gain_ffn)), full(row(shift_ffn))]
    hidden, normed, low_own, partial, act_own, slope_own = call(
        feed_own, (steps,),
        [full(x), full(ctx_own), full(ctx_oth), full(w_proj), proj_oth, full(row(b_proj)),
         full(row(gain_attn)), full(row(shift_attn)), full(row(b_down))] + own_up,
        [token(F32), token(F32), token(BF), token(F32), unit_out(BF), unit_out(F32)],
        micros=9.0,
    )
    normed_partner = swap_mp(normed)
    second_far = after(second_far, normed)
    up_oth = join(second, second_x, second_z, *second_far)
    third_x, third_z = after((third_x, third_z), normed)
    third_far = far_pieces(third_x, third_z)
    down_oth = join(third, third_x, third_z, *third_far)
    oth_up = [unit_col(up_oth), unit_row(bu_oth), unit_col(down_oth)]
    act_oth, slope_oth, out_own, d_summed, dffn_own, stats_ffn = call(
        feed_other, (steps,),
        [full(low_own), full(partial)] + oth_up + ffn_norm + [full(cot)],
        [unit_out(BF), unit_out(F32), token(BF), token(F32), token(BF), stat],
        [total], micros=9.0,
    )
    low_partner, act_partner, slope_partner, out_partner, dffn_partner = call(
        feed_partner, (steps,),
        [full(normed_partner)] + own_up + oth_up + ffn_norm + [full(row(b_down)), full(cot_partner)],
        [token(BF), unit_out(BF), unit_out(F32), token(BF), token(BF)],
        [total], micros=12.0,
    )
    outputs = both_sequences(place_m, out_own, out_partner, BF)

    split = dp == 16
    core_arg = jnp.reshape(core, (1,)).astype(jnp.int32)
    lead = (2, dp // 8, 2, width // dp)
    turned = pltpu.VMEM((width, LENGTH), BF)

    def gradient(kernels, lefts, rights, halves, block, start, count):
        cols = count * block
        ins = [full(array) for array in lefts] + [
            (array, (LENGTH, block), lambda i: (0, i + start)) for array in rights
        ]
        scratch = [turned] * len(lefts)
        micros = cols / 180
        if split:
            shape = halves + lead
            out = (shape + (cols,), F32, shape + (block,), lambda i: (0,) * len(shape) + (i,))
            ins = [(core_arg, "smem", None)] + ins
            return call(kernels[0], (count,), ins, [out] * 2, scratch, micros)
        out = ((width, cols), F32, (width, block), lambda i: (0, i))
        return call(kernels[1], (count,), ins, [out] * (1 + len(halves)), scratch, micros)

    def of_halves(left, own_right, oth_right, block, start=0, count=None):
        count = count or own_right.shape[1] // block
        kernels = (gradient_halves, plain_halves)
        return gradient(kernels, (left,), (own_right, oth_right), (2,), block, start, count)

    def of_tokens(lefts, rights, block, start, count):
        return gradient((gradient_tokens, plain_tokens), lefts, rights, (), block, start, count)

    bits = {"x": (d // 2) % 2, "l": (d // 4) % 2, "u": d // 8}
    hops = {"x": 2, "l": 4, "u": 8}

    class Reduction:
        def __init__(self, parts, order):
            self.names = ["h"] * ("h" in order) + ["u", "l", "x"]
            self.order, self.parts, self.terms = list(order), parts, None

        def step(self):
            if not split:
                return self.parts[0]
            if self.terms is None:
                got = swap_dp(self.parts[1], 1)
                self.terms = [self.parts[0], got]
                return got
            stage = self.order.pop(0)
            axis = self.names.index(stage)
            self.names.pop(axis)
            bit = 0 if stage == "h" else bits[stage]
            send = sum(pick(term, 1 - bit, axis) for term in self.terms)
            got = swap_mp(send) if stage == "h" else swap_dp(send, hops[stage])
            self.terms = [pick(term, bit, axis) for term in self.terms] + [got]
            return got

        def result(self):
            if not split:
                whole = self.parts[0]
                if len(self.parts) > 1:
                    whole = whole + swap_mp(self.parts[1])
                return lax.psum_scatter(whole, "dp", scatter_dimension=0, tiled=True)
            while self.order:
                self.step()
            return sum(self.terms)

    def everyone(vector):
        if not split:
            return lax.psum(vector, "dp")
        for bit in (1, 2, 4, 8):
            vector = vector + swap_dp(vector, bit)
        return vector

    chunk = units // 2 // 384

    def token_gradient(lefts, rights, at):
        return Reduction(of_tokens(lefts, rights, 384, at * chunk, chunk), "xlu")

    down = [
        token_gradient((dffn_own, dffn_partner), (act_own, act_partner), at) for at in range(2)
    ]
    down_cores = [one.step() for one in down]
    down_x = [one.step() for one in down]
    dffn_own, dffn_partner = after((dffn_own, dffn_partner), *down_cores)
    dup_own, dup_partner, sums_up, d_hidden, d_attn, dctx_own, dctx_oth, stats_attn = call(
        feed_backward, (steps,),
        [full(dffn_own), full(dffn_partner), unit_col(slope_own), unit_col(slope_oth),
         unit_col(slope_partner), unit_block(w_down), unit_col(down_oth), unit_col(w_up),
         unit_col(up_oth), full(d_summed), full(hidden), full(row(gain_attn)), full(w_proj),
         proj_oth],
        [unit_out(BF), unit_out(BF), ((8, units), F32, (8, UNIT_BLOCK), lambda i: (0, i)),
         token(F32), token(BF), (lanes, BF, None, None), (lanes, BF, None, None), stat],
        [total], micros=16.0,
    )
    dup_own, dup_partner = after((dup_own, dup_partner), down_x[0])
    down_l = [down[0].step()]
    up = [token_gradient((low_own, low_partner), (dup_own, dup_partner), at) for at in range(2)]
    proj = Reduction(of_halves(d_attn, ctx_own, ctx_oth, half), "hxlu")
    up_cores = [one.step() for one in up]
    proj_core = proj.step()
    down_l.append(down[1].step())
    up_x = [one.step() for one in up]

    def attend_back(q, k, v, lse, dctx):
        return call(
            attend_backward, (1,),
            [full(q), full(k), full(v), full(lse), full(dctx)] + masks,
            [((LENGTH, 3 * half), BF, None, None), ((8, 3 * half), F32, None, None)],
            [square], micros=7.0,
        )

    (dctx_own,) = after((dctx_own,), *up_cores, down_x[1], down_l[0], proj_core)
    dqkv_own, sums_own = attend_back(q_own, k_own, v_own, lse_own, dctx_own)
    down_u = [down[0].step()]
    proj_h = proj.step()
    (dctx_oth,) = after((dctx_oth,), dqkv_own, down_l[1])
    dqkv_oth, sums_oth = attend_back(q_oth, k_oth, v_oth, lse_oth, dctx_oth)
    down_u.append(down[1].step())
    up_l = [up[0].step()]
    (d_hidden,) = after((d_hidden,), up_x[0], proj_h, down_u[0])
    (grad_x,) = call(
        input_gradient, (1,),
        [full(d_hidden), full(dqkv_own), full(dqkv_oth)] + own_qkv + oth_qkv,
        [token(F32)], micros=5.5,
    )
    grad_x_theirs = swap_mp(grad_x)
    (x_late,) = after((x,), grad_x, up_x[1])
    up_l.append(up[1].step())
    qkv = [
        Reduction(of_halves(x_late, dqkv_own, dqkv_oth, half, at, 1), order)
        for at, order in enumerate(("xluh", "xluh", "luxh"))
    ]
    query_part, key_part, value_part = [one.result() for one in qkv]
    down_parts = [one.result() for one in down]
    up_parts = [one.result() for one in up]
    proj_part = proj.result()

    def ends(sums):
        return jnp.concatenate([sums[:1, :half], sums[:1, 2 * half:]], axis=1)

    common = jnp.concatenate([stats_ffn[:3], stats_attn[:3]], axis=0)
    mine = jnp.concatenate([common, ends(sums_own)], axis=0)
    theirs = jnp.concatenate([common, ends(sums_oth)], axis=0)
    sums = jnp.concatenate([mine + swap_mp(theirs), sums_up[0].reshape(-1, width)], axis=0)
    sums = everyone(sums)

    grad_inputs = both_sequences(place_m, grad_x, grad_x_theirs, F32)
    grad_up = jnp.concatenate(up_parts, axis=1)
    grad_down = jnp.concatenate(down_parts, axis=1).T
    return (
        outputs,
        grad_inputs,
        query_part,
        key_part,
        value_part,
        sums[6, :half],
        sums[6, half:],
        proj_part.T,
        sums[5],
        sums[3],
        sums[4],
        grad_up,
        sums[7:].reshape(-1),
        grad_down,
        sums[2],
        sums[0],
        sums[1],
    )


def solution(mesh):
    placed = (
        P("dp", None), P("dp"), P("dp"), P(None, "mp"), P(None, "mp"), P(None, "mp"), P("mp"),
        P("mp"), P("mp", None), P(), P(), P(), P(None, "mp"), P("mp"), P("mp", None), P(), P(), P(),
        P("dp", None),
    )
    return jax.shard_map(
        functools.partial(on_device, mesh.shape["dp"]),
        mesh=mesh,
        in_specs=placed,
        out_specs=(
            P("dp", None), P("dp", None), P("dp", "mp"), P("dp", "mp"), P("dp", "mp"), P("mp"),
            P("mp"), P("mp", "dp"), P(), P(), P(), P("dp", "mp"), P("mp"), P("mp", "dp"), P(), P(),
            P(),
        ),
        check_vma=False,
    )
```

```python
import functools
import math

import jax
import jax.numpy as jnp
from jax import lax
from jax.experimental import pallas as pl
from jax.experimental.pallas import tpu as pltpu
from jax.sharding import PartitionSpec as P

HD = 64
LENGTH = 512
QUERY_CHUNK = 256
UNIT_BLOCK = 512
BACK_BLOCK = 256
norm_eps = 1e-05
masked_value = -1000000000.0
BF = jnp.bfloat16
F32 = jnp.float32
VMEM_BYTES = 50 * 1024 * 1024


def nn(a, b):
    return lax.dot_general(a, b, (((1,), (0,)), ((), ())), preferred_element_type=F32)


def nt(a, b):
    return lax.dot_general(a, b, (((1,), (1,)), ((), ())), preferred_element_type=F32)


def call(body, grid, ins, outs, scratch=(), micros=1.0, alias=None):
    def spec(shape, block, index):
        if block == "smem":
            return pl.BlockSpec(memory_space=pltpu.SMEM)
        if block == "any":
            return pl.BlockSpec(memory_space=pl.ANY)
        if block is None:
            return pl.BlockSpec(shape, lambda *_: (0,) * len(shape))
        return pl.BlockSpec(block, index)

    moved = sum(a.size * a.dtype.itemsize for a, _, _ in ins)
    moved += sum(math.prod(s) * jnp.dtype(d).itemsize for s, d, _, _ in outs)
    return pl.pallas_call(
        body,
        grid=grid,
        in_specs=[spec(a.shape, b, i) for a, b, i in ins],
        out_specs=[spec(s, b, i) for s, _, b, i in outs],
        out_shape=[jax.ShapeDtypeStruct(s, d) for s, d, _, _ in outs],
        scratch_shapes=list(scratch),
        input_output_aliases=alias or {},
        compiler_params=pltpu.CompilerParams(vmem_limit_bytes=VMEM_BYTES),
        cost_estimate=pl.CostEstimate(
            flops=int(micros * 1.15e9), bytes_accessed=moved, transcendentals=0
        ),
    )(*[a for a, _, _ in ins])


def mask_bias(segc_ref, segr_ref, padc_ref, bias_ref):
    shape = bias_ref.shape
    key = lax.broadcasted_iota(jnp.int32, shape, 0)
    query = lax.broadcasted_iota(jnp.int32, shape, 1)
    same = segc_ref[...] == segr_ref[...]
    allowed = same & ((padc_ref[...] == 0) | (key == query))
    bias_ref[...] = jnp.where(allowed, 0.0, masked_value)


def attend_forward(
    x_ref, wq_ref, wk_ref, wv_ref, bq_ref, bv_ref, bu_ref, segc_ref, segr_ref, padc_ref,
    q_ref, k_ref, v_ref, ctx_ref, send_ref, lse_ref, bias_ref,
):
    x = x_ref[...]
    q_ref[...] = ((nn(x, wq_ref[...]) + bq_ref[...]).astype(BF).astype(F32) * HD ** (-0.5)).astype(BF)
    k_ref[...] = nn(x, wk_ref[...]).astype(BF)
    v_ref[...] = (nn(x, wv_ref[...]) + bv_ref[...]).astype(BF)
    mask_bias(segc_ref, segr_ref, padc_ref, bias_ref)
    length, wide = x.shape[0], q_ref.shape[1]
    if send_ref.shape[0] > length:
        send_ref[length:] = jnp.zeros((send_ref.shape[0] - length, wide), F32)
        for at in range(bu_ref.shape[1] // wide):
            send_ref[length + at:length + at + 1] = bu_ref[:, at * wide:(at + 1) * wide]

    def pair(index, carry):
        cols = pl.ds(pl.multiple_of(index * 128, 128), 128)
        keys = k_ref[:, cols]
        values_t = v_ref[:, cols].T
        lane = lax.broadcasted_iota(jnp.int32, (QUERY_CHUNK, 128), 1)
        for start in range(0, length, QUERY_CHUNK):
            rows = pl.ds(start, QUERY_CHUNK)
            query = q_ref[rows, cols]
            parts = []
            for head in range(2):
                one = jnp.where((lane < HD) == (head == 0), query, jnp.zeros_like(query))
                scores = nt(keys, one) + bias_ref[:, rows]
                highest = jnp.max(scores, axis=0, keepdims=True)
                grown = jnp.exp(scores - highest)
                total = jnp.sum(grown, axis=0, keepdims=True)
                weights = (grown * (1.0 / total)).astype(BF)
                lse_ref[pl.ds(2 * index + head, 1), rows] = highest + jnp.log(total)
                parts.append(nn(values_t[head * HD:(head + 1) * HD], weights))
            context = jnp.concatenate(parts, axis=0).T.astype(BF)
            ctx_ref[rows, cols] = context
            send_ref[rows, cols] = context.astype(F32)
        return carry

    lax.fori_loop(0, q_ref.shape[1] // 128, pair, 0)


def attend_backward(
    parts, q_ref, k_ref, v_ref, lse_ref, dctx_ref, segc_ref, segr_ref, padc_ref, wq_ref, wk_ref, wv_ref, *rest
):
    bias_ref, part_refs = rest[-1], rest[-1 - parts:-1]
    dqkv_ref, sums_ref = rest[-3 - parts:-1 - parts]
    mask_bias(segc_ref, segr_ref, padc_ref, bias_ref)
    length, width = q_ref.shape

    def pair(index, carry):
        first = pl.multiple_of(index * 128, 128)
        cols = pl.ds(first, 128)
        keys = k_ref[:, cols]
        values = v_ref[:, cols]
        keys_t = keys.T
        lane = lax.broadcasted_iota(jnp.int32, (QUERY_CHUNK, 128), 1)
        d_keys = [None, None]
        d_values = [None, None]
        for start in range(0, length, QUERY_CHUNK):
            rows = pl.ds(start, QUERY_CHUNK)
            query = q_ref[rows, cols]
            grad = dctx_ref[rows, cols]
            d_query = []
            for head in range(2):
                here = (lane < HD) == (head == 0)
                scores = nt(keys, jnp.where(here, query, jnp.zeros_like(query))) + bias_ref[:, rows]
                prob = jnp.exp(scores - lse_ref[pl.ds(2 * index + head, 1), rows])
                weights = prob.astype(BF)
                d_prob = nt(values, jnp.where(here, grad, jnp.zeros_like(grad)))
                inner = jnp.sum(prob * d_prob, axis=0, keepdims=True)
                raw = (prob * (d_prob - inner)).astype(BF)
                dv = nn(weights, grad)
                dk = nn(raw, query)
                d_values[head] = dv if start == 0 else d_values[head] + dv
                d_keys[head] = dk if start == 0 else d_keys[head] + dk
                d_query.append(nn(keys_t[head * HD:(head + 1) * HD], raw))
            dq = (jnp.concatenate(d_query, axis=0).T * HD ** (-0.5)).astype(BF)
            dqkv_ref[rows, cols] = dq
        full = lax.broadcasted_iota(jnp.int32, (length, 128), 1) < HD
        dqkv_ref[:, pl.ds(pl.multiple_of(width + first, 128), 128)] = jnp.where(
            full, d_keys[0], d_keys[1]
        ).astype(BF)
        dqkv_ref[:, pl.ds(pl.multiple_of(2 * width + first, 128), 128)] = jnp.where(
            full, d_values[0], d_values[1]
        ).astype(BF)
        return carry

    lax.fori_loop(0, width // 128, pair, 0)
    sums_ref[...] = jnp.broadcast_to(
        jnp.sum(dqkv_ref[...].astype(F32), axis=0, keepdims=True), sums_ref.shape
    )
    total = None
    for part, weight in enumerate((wq_ref, wk_ref, wv_ref)):
        term = nt(dqkv_ref[:, part * width:(part + 1) * width], weight[...])
        total = term if total is None else total + term
    at = 0
    for part_ref in part_refs:
        part_ref[...] = total[at:at + part_ref.shape[0]]
        at += part_ref.shape[0]


def moments(values):
    average = jnp.mean(values, axis=-1, keepdims=True)
    centered = values - average
    variance = jnp.mean(centered * centered, axis=-1, keepdims=True)
    inverse = lax.rsqrt(variance + norm_eps)
    return centered * inverse, inverse


def norm_backward(upstream, n, inverse, gain):
    scaled = upstream * gain
    return inverse * (
        scaled
        - jnp.mean(scaled, axis=-1, keepdims=True)
        - n * jnp.mean(scaled * n, axis=-1, keepdims=True)
    )


def down_sum(values):
    return jnp.sum(values, axis=0, keepdims=True)


def activate(nlow, wu_ref, bias, act_ref, slope_ref):
    up = nn(nlow, wu_ref[...]) + bias
    cdf = 0.5 * (1.0 + lax.erf(up * 2.0 ** (-0.5)))
    active = (up * cdf).astype(BF)
    act_ref[...] = active
    slope = cdf + up * jnp.exp(-0.5 * up * up) * (1.0 / math.sqrt(2.0 * math.pi))
    slope_ref[...] = slope.astype(BF)
    return active


def feed_own(
    x_ref, co_ref, cx_ref, wpo_ref, wpx_ref, bp_ref, g_ref, s_ref, bd_ref, wu_ref, bu_ref, wd_ref, *rest
):
    nlow_ref, acc_ref, hid_ref, act_ref, slope_ref = rest[-5:]

    @pl.when(pl.program_id(0) == 0)
    def _():
        attn = nn(co_ref[...], wpo_ref[...]) + nt(cx_ref[:x_ref.shape[0]].astype(BF), wpx_ref[...]) + bp_ref[...]
        hidden = x_ref[...].astype(F32) + attn
        hid_ref[...] = hidden
        n, _ = moments(hidden)
        normed = n * g_ref[...] + s_ref[...]
        nlow_ref[...] = normed.astype(BF)
        acc_ref[...] = normed + bd_ref[...]

    acc_ref[...] += nn(activate(nlow_ref[...], wu_ref, bu_ref[...], act_ref, slope_ref), wd_ref[...])


def feed_up(nlow_ref, wu_ref, bu_ref, *rest):
    bias = bu_ref[pl.ds(pl.program_id(0), 1), :]
    activate(nlow_ref[...], wu_ref, bias, *rest[-2:])


def feed_down(
    act_ref, starta_ref, startb_ref, wd_ref, g_ref, s_ref, cot_ref,
    out_ref, dsum_ref, dffn_ref, stats_ref, low_ref,
):
    weights = wd_ref[...].astype(BF)
    low_ref[...] = weights
    stats_ref[...] = jnp.zeros_like(stats_ref)
    length = starta_ref.shape[0]
    for at, start_ref in enumerate((starta_ref, startb_ref)):
        rows = pl.ds(at * length, length)
        total = start_ref[...] + nt(act_ref[rows, :], weights)
        n, inverse = moments(total)
        out_ref[rows, :] = (n * g_ref[...] + s_ref[...]).astype(BF)
        cot = cot_ref[rows, :].astype(F32)
        d_summed = norm_backward(cot, n, inverse, g_ref[...])
        d_ffn = d_summed.astype(BF)
        dsum_ref[rows, :] = d_summed
        dffn_ref[rows, :] = d_ffn
        stats_ref[0:1] += down_sum(cot * n)
        stats_ref[1:2] += down_sum(cot)
        stats_ref[2:3] += down_sum(d_ffn.astype(F32))


def feed_backward(
    dffn_ref, so_ref, sx_ref, wdo_ref, wdx_ref, wuo_ref, wux_ref, dsum_ref, hid_ref, g_ref, wpo_ref,
    duo_ref, bup_ref, dhid_ref, dattn_ref, dctx_ref, stats_ref, acc_ref,
):
    @pl.when(pl.program_id(0) == 0)
    def _():
        acc_ref[...] = dsum_ref[...]

    d_ffn = dffn_ref[...]
    d_own = (nt(d_ffn, wdo_ref[...]) * so_ref[...].astype(F32)).astype(BF)
    d_other = (nn(d_ffn, wdx_ref[...]) * sx_ref[...].astype(F32)).astype(BF)
    duo_ref[...] = d_own
    bup_ref[...] = jnp.broadcast_to(down_sum(d_own.astype(F32)), bup_ref.shape)
    acc_ref[...] += nt(d_own, wuo_ref[...]) + nt(d_other, wux_ref[...])

    @pl.when(pl.program_id(0) == pl.num_programs(0) - 1)
    def _():
        d_normed = acc_ref[...]
        n, inverse = moments(hid_ref[...])
        d_hidden = norm_backward(d_normed, n, inverse, g_ref[...])
        d_attn = d_hidden.astype(BF)
        dhid_ref[...] = d_hidden
        dattn_ref[...] = d_attn
        dctx_ref[...] = nt(d_attn, wpo_ref[...]).astype(BF)
        stats_ref[...] = jnp.zeros_like(stats_ref)
        stats_ref[0:1] = down_sum(d_normed * n)
        stats_ref[1:2] = down_sum(d_normed)
        stats_ref[2:3] = down_sum(d_attn.astype(F32))


def input_total(parts, dhid_ref, *refs):
    at = 0
    for mine_ref, theirs_ref in zip(refs[:parts], refs[parts:2 * parts]):
        rows = pl.ds(at, mine_ref.shape[0])
        refs[-1][rows, :] = dhid_ref[rows, :] + (mine_ref[...] + theirs_ref[...])
        at += mine_ref.shape[0]


def scatter_rows(g, first, keep_ref, send_ref, rows, extra=None):
    over, across = keep_ref.shape[1:3]
    for block in range(keep_ref.shape[0] * over * across):
        at = 2 * block * rows
        even, odd = g[at:at + rows], g[at + rows:at + 2 * rows]
        place = (block // (over * across), block // across % over, block % across)
        keep_ref[place + (slice(0, rows),)] = jnp.where(first, even, odd)
        send_ref[place + (slice(0, rows),)] = jnp.where(first, odd, even)
        if extra is not None:
            keep_ref[place + (slice(rows, None),)] = extra
            send_ref[place + (slice(rows, None),)] = extra


def put(g, core_ref, outs, rows, extra=None):
    if len(outs) == 2:
        scatter_rows(g, core_ref[0] == 0, *outs, rows, extra)
    else:
        outs[0][:g.shape[0]] = g
        if extra is not None:
            outs[0][g.shape[0]:] = extra


def turn(refs, turned, step=0):
    @pl.when(pl.program_id(0) == step)
    def _():
        at = 0
        for ref in refs:
            turned[:, at:at + ref.shape[0]] = ref[...].T
            at += ref.shape[0]


def gradient(left_ref, right_ref, out_ref, turned):
    turn((left_ref,), turned)
    out_ref[...] = nn(turned[...], right_ref[...])


def gradient_up(rows, core_ref, la_ref, lb_ref, right_ref, proj_ref, ca_ref, cb_ref, *rest):
    turned, outs = rest[-1], rest[:-1]
    last = pl.num_programs(0) - 1
    count = len(outs) // 2
    length = la_ref.shape[0]
    turn((la_ref, lb_ref), turned)
    turn((proj_ref,), turned, last)

    @pl.when(pl.program_id(0) < last // 2)
    def _():
        put(nn(turned[...], right_ref[...]), core_ref, outs[:count], rows)

    @pl.when((pl.program_id(0) >= last // 2) & (pl.program_id(0) < last))
    def _():
        put(nn(turned[...], right_ref[...]), core_ref, outs[count:], rows)

    @pl.when(pl.program_id(0) == last)
    def _():
        g = nn(turned[:, :length], ca_ref[...]) + nn(turned[:, length:], cb_ref[...])
        put(g, core_ref, outs[count:], rows)


def gradient_attention(
    rows, core_ref, x_ref, dqkv_ref, f_ref, a_ref, up_ref, ka_ref, kb_ref, *rest
):
    turned, outs = rest[-1], rest[:-1]
    count = len(outs) // 2
    width = x_ref.shape[1]
    half = width // 2
    up, qkv = up_ref[...], ka_ref[...] + kb_ref[...]
    pieces = [f_ref[:3], a_ref[:3]] + [
        up[:1, at * width:(at + 1) * width] for at in range(up.shape[1] // width)
    ] + [jnp.concatenate([qkv[:1, :half], qkv[:1, 2 * half:]], axis=1)]
    have = sum(piece.shape[0] for piece in pieces)
    pieces.append(jnp.zeros((-have % 16, width), F32))
    extra = jnp.concatenate(pieces, axis=0)
    turn((x_ref,), turned)
    put(nn(turned[...], dqkv_ref[:, :2 * half]), core_ref, outs[:count], rows, extra)
    put(nn(turned[...], dqkv_ref[:, 2 * half:]), core_ref, outs[count:], rows)


def join_pieces(place_ref, *refs):
    out_ref = refs[-1]
    rows = refs[0].shape[0]
    for mine in (True, False):
        base = (place_ref[0] if mine else 1 - place_ref[0]) * 4
        pieces = refs[:5] if mine else refs[5:10]
        starts = [base + jnp.bitwise_xor(place_ref[1], piece) for piece in (0, 1, 2, 3, 3)]
        for index, (at, piece) in enumerate(zip(starts, pieces)):
            start = at * rows + (rows // 2 if index == 4 else 0)
            out_ref[pl.ds(pl.multiple_of(start, 16), piece.shape[0])] = piece[...].astype(BF)


def pick(array, index, axis):
    return lax.dynamic_index_in_dim(array, index, axis, keepdims=False)


def lock(*values):
    return lax.optimization_barrier(values)


def on_device(
    dp, inputs, segment_ids, pad_flags, w_query, w_key, w_value, b_query, b_value, w_proj, b_proj,
    gain_attn, shift_attn, w_up, b_up, w_down, b_down, gain_ffn, shift_ffn, cotangent,
):
    d = lax.axis_index("dp")
    tokens, width = inputs.shape
    half = w_query.shape[1]
    units = w_up.shape[1]
    core, low = d % 2, (d // 2) % 4
    pair = range(tokens // LENGTH)

    def swap_mp(array):
        return lax.ppermute(array, "mp", [(0, 1), (1, 0)])

    def swap_dp(array, bit):
        return lax.ppermute(array, "dp", [(i, i ^ bit) for i in range(dp)])

    def row(vector):
        return vector.reshape(1, -1)

    full = lambda array: (array, None, None)

    rows = width // 8
    place_d = jnp.stack([core, low]).astype(jnp.int32)

    def eighth(weight):
        return lax.dynamic_slice_in_dim(weight, (core * 4 + low) * rows, rows, 0).astype(F32)

    def eighth_t(weight):
        return lax.dynamic_slice_in_dim(weight, (core * 4 + low) * rows, rows, 1).T.astype(F32)

    def near_pieces(own):
        return swap_dp(own, 2), swap_dp(own, 4)

    def far_pieces(by_x, by_z):
        return swap_dp(by_z[:rows // 2], 2), swap_dp(by_x[rows // 2:], 4)

    def join(mine, theirs):
        (joined,) = call(
            join_pieces, (1,), [(place_d, "smem", None)] + [full(a) for a in mine + theirs],
            [((width, mine[0].shape[1]), BF, None, None)],
            micros=3.0,
        )
        return joined

    def other_core(pieces):
        return tuple(swap_dp(piece, 1) for piece in pieces)

    def tokens_of(array, at):
        return lax.slice_in_dim(array, at * LENGTH, (at + 1) * LENGTH, axis=0)

    def sequence(array, at):
        return (array, (LENGTH, array.shape[1]), lambda *_: (at, 0))

    square = pltpu.VMEM((LENGTH, LENGTH), F32)
    heads = half // HD
    lanes = (LENGTH, half)
    masks = []
    for at in pair:
        seg, pad = tokens_of(segment_ids, at), tokens_of(pad_flags, at)
        masks.append([full(seg.reshape(-1, 1)), full(row(seg)), full(pad.reshape(-1, 1))])
    own_qkv = [full(w_query), full(w_key), full(w_value)]

    def attend(at, token):
        return call(
            attend_forward, (1,),
            [sequence(token, at)] + own_qkv + [full(row(b_query)), full(row(b_value)), full(row(b_up))]
            + masks[at],
            [(lanes, BF, None, None)] * 4
            + [((LENGTH + 8 * (at == 0), half), F32, None, None), ((heads, LENGTH), F32, None, None)],
            [square], micros=9.0,
        )

    shard = width // dp
    (proj,) = lock(swap_mp(eighth_t(w_proj)))
    down_y = swap_mp(lax.dynamic_slice_in_dim(w_down, d * shard, shard, 1).T.astype(F32))
    saved = [attend(0, lock(inputs, proj)[0])]
    proj, proj_near, up, down_y, saved[0] = lock(
        proj, near_pieces(proj), swap_mp(lock(eighth(w_up), proj)[0]), down_y, tuple(saved[0])
    )
    down_oth = lax.all_gather(down_y, "dp", axis=0, tiled=True)
    saved.append(attend(1, lock(inputs, proj)[0]))
    proj = (proj,) + tuple(proj_near)
    proj_far = far_pieces(*proj_near)
    ctx_a, up_near, proj_far, proj_core, saved[1] = lock(
        swap_mp(saved[0][4]), near_pieces(up), proj_far, other_core(proj), tuple(saved[1])
    )
    proj_far, proj_far_core, proj, proj_core = lock(
        proj_far, other_core(proj_far), proj, proj_core
    )

    steps = units // UNIT_BLOCK
    unit_row = lambda array: (array, (1, UNIT_BLOCK), lambda i: (0, i))
    unit_col = lambda array: (array, (array.shape[0], UNIT_BLOCK), lambda i: (0, i))
    unit_block = lambda array: (array, (UNIT_BLOCK, width), lambda i: (i, 0))
    unit_all = lambda array, block: (array, (array.shape[0], block), lambda i: (0, i))
    column = lambda array: (array, (array.shape[0], half), lambda i: (0, i))
    token = lambda dtype: ((LENGTH, width), dtype, None, None)
    stat = ((8, width), F32, None, None)
    def rows_of(at, cols, dtype, block=None):
        if block is None:
            return ((tokens, cols), dtype, (LENGTH, cols), lambda *_: (at, 0))
        return ((tokens, cols), dtype, (LENGTH, block), lambda i: (at, i))

    proj_oth = join(proj + tuple(proj_far), proj_core + tuple(proj_far_core))

    def forward_own(at, context, before):
        outs = call(
            feed_own, (steps,),
            [sequence(inputs, at), full(saved[at][3]), full(context), full(w_proj), full(proj_oth),
             full(row(b_proj)), full(row(gain_attn)), full(row(shift_attn)), full(row(b_down)),
             unit_col(w_up), unit_row(row(b_up)), unit_block(w_down)]
            + [(array, "any", None) for array in before],
            [token(BF), token(F32), rows_of(at, width, F32), rows_of(at, units, BF, UNIT_BLOCK),
             rows_of(at, units, BF, UNIT_BLOCK)],
            micros=8.0, alias={12 + i: 2 + i for i in range(len(before))},
        )
        return outs[0], outs[1], outs[2:]

    def forward_other(at, normed, before):
        return call(
            feed_up, (units // half,),
            [full(normed), column(joined), (ctx_a, (8, half), lambda i: (LENGTH // 8, 0))]
            + [(array, "any", None) for array in before],
            [rows_of(at, units, BF, half)] * 2, micros=4.0,
            alias={3 + i: i for i in range(len(before))},
        )

    normed_a, partial_a, kept = forward_own(0, ctx_a, ())
    up = (up,) + tuple(up_near)
    ctx_b, up_far, up_core, normed_a, partial_a, kept = lock(
        swap_mp(saved[1][4]), far_pieces(*up_near), other_core(up), normed_a, partial_a, tuple(kept)
    )
    up, up_far, up_far_core, up_core, normed_a, ctx_b = lock(
        up, up_far, other_core(up_far), up_core, normed_a, ctx_b
    )
    joined = join(up + tuple(up_far), up_core + tuple(up_far_core))
    other = forward_other(0, normed_a, ())
    normed_b, partial_b, (hidden, act_own, slope_own) = forward_own(1, ctx_b, kept)
    act_oth, slope_oth = forward_other(1, normed_b, other)
    every = lambda dtype: ((tokens, width), dtype, None, None)
    outputs, d_summed, d_ffn, stats_ffn, down_oth = call(
        feed_down, (1,),
        [full(act_oth), full(partial_a), full(partial_b), full(down_oth), full(row(gain_ffn)),
         full(row(shift_ffn)), full(cotangent)],
        [every(BF), every(F32), every(BF), stat, ((width, units), BF, None, None)], micros=10.0,
    )

    split = dp == 16
    core_arg = jnp.reshape(core, (1,)).astype(jnp.int32)
    lead = (2, dp // 8, 2, width // dp)
    turned = pltpu.VMEM((width, tokens), BF)

    def parted(cols, block, index, extra=0):
        if not split:
            out = ((width + extra, cols), F32, (width + extra, block), lambda i: (0, index(i)))
            return [out]
        shape = lead[:-1] + (lead[-1] + extra,)
        return [(shape + (cols,), F32, shape + (block,), lambda i: (0, 0, 0, 0, index(i)))] * 2

    def pairs(outs):
        return outs[:len(outs) // 2], outs[len(outs) // 2:]

    bits = {"x": (d // 2) % 2, "l": (d // 4) % 2, "u": d // 8}
    hops = {"x": 2, "l": 4, "u": 8}

    class Reduction:
        def __init__(self, parts, order, terms=None):
            self.names = ["u", "l", "x"]
            self.order, self.parts, self.terms = list(order), parts, terms

        def step(self):
            if not split:
                return self.parts[0]
            if self.terms is None:
                got = swap_dp(self.parts[1], 1)
                self.terms = [self.parts[0], got]
                return got
            stage = self.order.pop(0)
            axis = self.names.index(stage)
            self.names.pop(axis)
            bit = bits[stage]
            send = sum(pick(term, 1 - bit, axis) for term in self.terms)
            got = swap_dp(send, hops[stage])
            self.terms = [pick(term, bit, axis) for term in self.terms] + [got]
            return got

        def result(self):
            if not split:
                return lax.psum_scatter(self.parts[0], "dp", scatter_dimension=0, tiled=True)
            while self.order:
                self.step()
            return sum(self.terms)

    (down_whole,) = call(
        gradient, (units // UNIT_BLOCK,), [full(d_ffn), unit_all(act_own, UNIT_BLOCK)],
        [((width, units), F32, (width, UNIT_BLOCK), lambda i: (0, i))], [turned], 6.0,
    )
    d_ffn, down_whole = lock(d_ffn, down_whole)
    down_part = lax.psum_scatter(down_whole, "dp", scatter_dimension=0, tiled=True)
    back = lambda array: (array, (array.shape[0], BACK_BLOCK), lambda i: (0, i))
    d_up, sums_up, d_hidden, d_attn, d_context, stats_attn = call(
        feed_backward, (units // BACK_BLOCK,),
        [full(d_ffn), back(slope_own), back(slope_oth),
         (w_down, (BACK_BLOCK, width), lambda i: (i, 0)), back(down_oth), back(w_up), back(joined),
         full(d_summed), full(hidden), full(row(gain_attn)), full(w_proj)],
        [((tokens, units), BF, (tokens, BACK_BLOCK), lambda i: (0, i)),
         ((8, units), F32, (8, BACK_BLOCK), lambda i: (0, i)), every(F32), every(BF),
         ((tokens, half), BF, None, None), stat],
        [pltpu.VMEM((tokens, width), F32)], micros=20.0,
    )

    def back_attend(at, grad, before, sizes):
        q, k, v, _, _, lse = saved[at]
        outs = call(
            functools.partial(attend_backward, len(sizes)), (1,),
            [full(q), full(k), full(v), full(lse), sequence(grad, at)] + masks[at] + own_qkv
            + [(array, "any", None) for array in before],
            [rows_of(at, 3 * half, BF), ((8, 3 * half), F32, None, None)]
            + [((size, width), F32, None, None) for size in sizes],
            [square], micros=9.0, alias={11: 0} if before else {},
        )
        return outs[0], outs[1], list(outs[2:])

    blocks = units // half
    up = call(
        functools.partial(gradient_up, lead[-1]), (blocks + 1,),
        [(core_arg, "smem", None), full(normed_a), full(normed_b),
         (d_up, (tokens, half), lambda i: (0, jnp.minimum(i, blocks - 1))), full(d_attn),
         full(saved[0][3]), full(saved[1][3])],
        parted(units // 2, half, lambda i: jnp.minimum(i, blocks // 2 - 1))
        + parted(units // 2 + half, half, lambda i: jnp.maximum(i - blocks // 2, 0)),
        [turned], 9.0,
    )
    up, d_context = lock(up, d_context)
    up = [Reduction(parts, order) for parts, order in zip(pairs(up), ("lux", "xlu"))]

    def advance(reductions, *values):
        for one in reductions:
            one.step()
        if not split:
            return lock(*values)
        terms, *values = lock([one.terms for one in reductions], *values)
        for one, changed in zip(reductions, terms):
            one.terms = list(changed)
        return values

    dqkv, sums_a, mine_a = back_attend(0, d_context, (), (256, 256))
    dqkv, mine_a, d_context = advance(up, dqkv, mine_a, d_context)
    theirs_a = [swap_mp(mine_a[0])]
    dqkv, sums_b, mine_b = back_attend(1, d_context, (dqkv,), (128, 256, 128))
    dqkv, mine_a, mine_b, theirs_a = advance(up, dqkv, mine_a, mine_b, theirs_a)
    theirs_a.append(swap_mp(mine_a[1]))
    last = call(
        functools.partial(gradient_attention, lead[-1]), (1,),
        [(core_arg, "smem", None), full(inputs), full(dqkv)]
        + [full(a) for a in (stats_ffn, stats_attn, sums_up, sums_a, sums_b)],
        parted(2 * half, 2 * half, lambda i: 0, 16) + parted(half, half, lambda i: 0),
        [turned], 7.0,
    )
    last, mine_b, theirs_a = advance(up, last, mine_b, theirs_a)
    query, value = [Reduction(parts, order) for parts, order in zip(pairs(last), ("xlu", "lux"))]
    theirs_b = []
    for moving in (up + [query, value], [query, value], [query, value]):
        theirs_b.append(swap_mp(mine_b[len(theirs_b)]))
        mine_b, theirs_b = advance(moving, mine_b, theirs_b)
    if split:
        query_part, value_part = query.result(), value.result()
        vectors = query_part[shard:]
    else:
        (whole,) = query.parts
        vectors = lax.psum(whole[width:], "dp")
        query_part = lax.psum_scatter(whole[:width], "dp", scatter_dimension=0, tiled=True)
        value_part = value.result()
    query_part = query_part[:shard]
    up_part = [one.result() for one in up]
    proj_part = up_part[1][:, units // 2:]
    up_part = jnp.concatenate([up_part[0], up_part[1][:, :units // 2]], axis=1)

    grad_inputs = None
    for at, (mine, theirs) in enumerate(((mine_a, theirs_a), (mine_b, theirs_b))):
        ins = [sequence(d_hidden, at)] + [full(a) for a in list(mine) + list(theirs)]
        before = len(ins)
        if grad_inputs is not None:
            ins.append((grad_inputs, "any", None))
        (grad_inputs,) = call(
            functools.partial(input_total, len(mine)), (1,), ins, [rows_of(at, width, F32)],
            micros=2.5, alias={} if at == 0 else {before: 0},
        )
    return (
        outputs,
        grad_inputs,
        query_part[:, :half],
        query_part[:, half:],
        value_part,
        vectors[8, :half],
        vectors[8, half:],
        proj_part.T,
        vectors[5],
        vectors[3],
        vectors[4],
        up_part,
        vectors[6:8].reshape(-1),
        down_part.T,
        vectors[2],
        vectors[0],
        vectors[1],
    )


def solution(mesh):
    placed = (
        P("dp", None), P("dp"), P("dp"), P(None, "mp"), P(None, "mp"), P(None, "mp"), P("mp"),
        P("mp"), P("mp", None), P(), P(), P(), P(None, "mp"), P("mp"), P("mp", None), P(), P(), P(),
        P("dp", None),
    )
    return jax.shard_map(
        functools.partial(on_device, mesh.shape["dp"]),
        mesh=mesh,
        in_specs=placed,
        out_specs=(
            P("dp", None), P("dp", None), P("dp", "mp"), P("dp", "mp"), P("dp", "mp"), P("mp"),
            P("mp"), P("mp", "dp"), P(), P(), P(), P("dp", "mp"), P("mp"), P("mp", "dp"), P(), P(),
            P(),
        ),
        check_vma=False,
    )
```

```python
import functools
import math

import jax
import jax.numpy as jnp
from jax import lax
from jax.experimental import pallas as pl
from jax.experimental.pallas import tpu as pltpu
from jax.sharding import PartitionSpec as P

HD = 64
LENGTH = 512
QUERY_CHUNK = 256
UNIT_BLOCK = 512
BACK_BLOCK = 256
UP_ORDERS = ("lux", "xlu")
LAST_ORDERS = ("xlu", "lux")
norm_eps = 1e-05
masked_value = -1000000000.0
BF = jnp.bfloat16
F32 = jnp.float32
VMEM_BYTES = 50 * 1024 * 1024


def nn(a, b):
    return lax.dot_general(a, b, (((1,), (0,)), ((), ())), preferred_element_type=F32)


def nt(a, b):
    return lax.dot_general(a, b, (((1,), (1,)), ((), ())), preferred_element_type=F32)


def call(body, grid, ins, outs, scratch=(), micros=1.0, alias=None):
    def spec(shape, block, index):
        if block == "smem":
            return pl.BlockSpec(memory_space=pltpu.SMEM)
        if block == "any":
            return pl.BlockSpec(memory_space=pl.ANY)
        if block is None:
            return pl.BlockSpec(shape, lambda *_: (0,) * len(shape))
        return pl.BlockSpec(block, index)

    moved = sum(a.size * a.dtype.itemsize for a, _, _ in ins)
    moved += sum(math.prod(s) * jnp.dtype(d).itemsize for s, d, _, _ in outs)
    return pl.pallas_call(
        body,
        grid=grid,
        in_specs=[spec(a.shape, b, i) for a, b, i in ins],
        out_specs=[spec(s, b, i) for s, _, b, i in outs],
        out_shape=[jax.ShapeDtypeStruct(s, d) for s, d, _, _ in outs],
        scratch_shapes=list(scratch),
        input_output_aliases=alias or {},
        compiler_params=pltpu.CompilerParams(vmem_limit_bytes=VMEM_BYTES),
        cost_estimate=pl.CostEstimate(
            flops=int(micros * 1.15e9), bytes_accessed=moved, transcendentals=0
        ),
    )(*[a for a, _, _ in ins])


def mask_bias(segc_ref, segr_ref, padc_ref, bias_ref):
    shape = bias_ref.shape
    key = lax.broadcasted_iota(jnp.int32, shape, 0)
    query = lax.broadcasted_iota(jnp.int32, shape, 1)
    same = segc_ref[...] == segr_ref[...]
    allowed = same & ((padc_ref[...] == 0) | (key == query))
    bias_ref[...] = jnp.where(allowed, 0.0, masked_value)


def attend_forward(
    x_ref, wq_ref, wk_ref, wv_ref, bq_ref, bv_ref, bu_ref, segc_ref, segr_ref, padc_ref,
    q_ref, k_ref, v_ref, ctx_ref, send_ref, lse_ref, bias_ref,
):
    x = x_ref[...]
    q_ref[...] = ((nn(x, wq_ref[...]) + bq_ref[...]).astype(BF).astype(F32) * HD ** (-0.5)).astype(BF)
    k_ref[...] = nn(x, wk_ref[...]).astype(BF)
    v_ref[...] = (nn(x, wv_ref[...]) + bv_ref[...]).astype(BF)
    mask_bias(segc_ref, segr_ref, padc_ref, bias_ref)
    length, wide = x.shape[0], q_ref.shape[1]
    if send_ref.shape[0] > length:
        send_ref[length:] = jnp.zeros((send_ref.shape[0] - length, wide), F32)
        for at in range(bu_ref.shape[1] // wide):
            send_ref[length + at:length + at + 1] = bu_ref[:, at * wide:(at + 1) * wide]

    def pair(index, carry):
        cols = pl.ds(pl.multiple_of(index * 128, 128), 128)
        keys = k_ref[:, cols]
        values_t = v_ref[:, cols].T
        lane = lax.broadcasted_iota(jnp.int32, (QUERY_CHUNK, 128), 1)
        for start in range(0, length, QUERY_CHUNK):
            rows = pl.ds(start, QUERY_CHUNK)
            query = q_ref[rows, cols]
            parts = []
            for head in range(2):
                one = jnp.where((lane < HD) == (head == 0), query, jnp.zeros_like(query))
                scores = nt(keys, one) + bias_ref[:, rows]
                highest = jnp.max(scores, axis=0, keepdims=True)
                grown = jnp.exp(scores - highest)
                total = jnp.sum(grown, axis=0, keepdims=True)
                weights = (grown * (1.0 / total)).astype(BF)
                lse_ref[pl.ds(2 * index + head, 1), rows] = highest + jnp.log(total)
                parts.append(nn(values_t[head * HD:(head + 1) * HD], weights))
            context = jnp.concatenate(parts, axis=0).T.astype(BF)
            ctx_ref[rows, cols] = context
            send_ref[rows, cols] = context.astype(F32)
        return carry

    lax.fori_loop(0, q_ref.shape[1] // 128, pair, 0)


def attend_backward(
    parts, q_ref, k_ref, v_ref, lse_ref, dctx_ref, segc_ref, segr_ref, padc_ref, wq_ref, wk_ref, wv_ref, *rest
):
    bias_ref, part_refs = rest[-1], rest[-1 - parts:-1]
    dqkv_ref, sums_ref = rest[-3 - parts:-1 - parts]
    mask_bias(segc_ref, segr_ref, padc_ref, bias_ref)
    length, width = q_ref.shape

    def pair(index, carry):
        first = pl.multiple_of(index * 128, 128)
        cols = pl.ds(first, 128)
        keys = k_ref[:, cols]
        values = v_ref[:, cols]
        keys_t = keys.T
        lane = lax.broadcasted_iota(jnp.int32, (QUERY_CHUNK, 128), 1)
        d_keys = [None, None]
        d_values = [None, None]
        for start in range(0, length, QUERY_CHUNK):
            rows = pl.ds(start, QUERY_CHUNK)
            query = q_ref[rows, cols]
            grad = dctx_ref[rows, cols]
            d_query = []
            for head in range(2):
                here = (lane < HD) == (head == 0)
                scores = nt(keys, jnp.where(here, query, jnp.zeros_like(query))) + bias_ref[:, rows]
                prob = jnp.exp(scores - lse_ref[pl.ds(2 * index + head, 1), rows])
                weights = prob.astype(BF)
                d_prob = nt(values, jnp.where(here, grad, jnp.zeros_like(grad)))
                inner = jnp.sum(prob * d_prob, axis=0, keepdims=True)
                raw = (prob * (d_prob - inner)).astype(BF)
                dv = nn(weights, grad)
                dk = nn(raw, query)
                d_values[head] = dv if start == 0 else d_values[head] + dv
                d_keys[head] = dk if start == 0 else d_keys[head] + dk
                d_query.append(nn(keys_t[head * HD:(head + 1) * HD], raw))
            dq = (jnp.concatenate(d_query, axis=0).T * HD ** (-0.5)).astype(BF)
            dqkv_ref[rows, cols] = dq
        full = lax.broadcasted_iota(jnp.int32, (length, 128), 1) < HD
        dqkv_ref[:, pl.ds(pl.multiple_of(width + first, 128), 128)] = jnp.where(
            full, d_keys[0], d_keys[1]
        ).astype(BF)
        dqkv_ref[:, pl.ds(pl.multiple_of(2 * width + first, 128), 128)] = jnp.where(
            full, d_values[0], d_values[1]
        ).astype(BF)
        return carry

    lax.fori_loop(0, width // 128, pair, 0)
    sums_ref[...] = jnp.broadcast_to(
        jnp.sum(dqkv_ref[...].astype(F32), axis=0, keepdims=True), sums_ref.shape
    )
    total = None
    for part, weight in enumerate((wq_ref, wk_ref, wv_ref)):
        term = nt(dqkv_ref[:, part * width:(part + 1) * width], weight[...])
        total = term if total is None else total + term
    at = 0
    for part_ref in part_refs:
        part_ref[...] = total[at:at + part_ref.shape[0]]
        at += part_ref.shape[0]


def moments(values):
    average = jnp.mean(values, axis=-1, keepdims=True)
    centered = values - average
    variance = jnp.mean(centered * centered, axis=-1, keepdims=True)
    inverse = lax.rsqrt(variance + norm_eps)
    return centered * inverse, inverse


def norm_backward(upstream, n, inverse, gain):
    scaled = upstream * gain
    return inverse * (
        scaled
        - jnp.mean(scaled, axis=-1, keepdims=True)
        - n * jnp.mean(scaled * n, axis=-1, keepdims=True)
    )


def down_sum(values):
    return jnp.sum(values, axis=0, keepdims=True)


def activate(nlow, wu_ref, bias, act_ref, slope_ref):
    up = nn(nlow, wu_ref[...]) + bias
    cdf = 0.5 * (1.0 + lax.erf(up * 2.0 ** (-0.5)))
    active = (up * cdf).astype(BF)
    act_ref[...] = active
    slope = cdf + up * jnp.exp(-0.5 * up * up) * (1.0 / math.sqrt(2.0 * math.pi))
    slope_ref[...] = slope.astype(BF)
    return active


def feed_own(
    x_ref, co_ref, cx_ref, wpo_ref, wpx_ref, bp_ref, g_ref, s_ref, bd_ref, wu_ref, bu_ref, wd_ref, *rest
):
    nlow_ref, acc_ref, hid_ref, act_ref, slope_ref = rest[-5:]

    @pl.when(pl.program_id(0) == 0)
    def _():
        attn = nn(co_ref[...], wpo_ref[...]) + nt(cx_ref[:x_ref.shape[0]].astype(BF), wpx_ref[...]) + bp_ref[...]
        hidden = x_ref[...].astype(F32) + attn
        hid_ref[...] = hidden
        n, _ = moments(hidden)
        normed = n * g_ref[...] + s_ref[...]
        nlow_ref[...] = normed.astype(BF)
        acc_ref[...] = normed + bd_ref[...]

    acc_ref[...] += nn(activate(nlow_ref[...], wu_ref, bu_ref[...], act_ref, slope_ref), wd_ref[...])


def feed_up(nlow_ref, wu_ref, bu_ref, *rest):
    bias = bu_ref[pl.ds(pl.program_id(0), 1), :]
    activate(nlow_ref[...], wu_ref, bias, *rest[-2:])


def feed_down(
    act_ref, starta_ref, startb_ref, wd_ref, g_ref, s_ref, cot_ref,
    out_ref, dsum_ref, dffn_ref, stats_ref, low_ref,
):
    weights = wd_ref[...].astype(BF)
    low_ref[...] = weights
    stats_ref[...] = jnp.zeros_like(stats_ref)
    length = starta_ref.shape[0]
    for at, start_ref in enumerate((starta_ref, startb_ref)):
        rows = pl.ds(at * length, length)
        total = start_ref[...] + nt(act_ref[rows, :], weights)
        n, inverse = moments(total)
        out_ref[rows, :] = (n * g_ref[...] + s_ref[...]).astype(BF)
        cot = cot_ref[rows, :].astype(F32)
        d_summed = norm_backward(cot, n, inverse, g_ref[...])
        d_ffn = d_summed.astype(BF)
        dsum_ref[rows, :] = d_summed
        dffn_ref[rows, :] = d_ffn
        stats_ref[0:1] += down_sum(cot * n)
        stats_ref[1:2] += down_sum(cot)
        stats_ref[2:3] += down_sum(d_ffn.astype(F32))


def feed_backward(
    dffn_ref, so_ref, sx_ref, wdo_ref, wdx_ref, wuo_ref, wux_ref, dsum_ref, hid_ref, g_ref, wpo_ref,
    duo_ref, bup_ref, dhid_ref, dattn_ref, dctx_ref, stats_ref, acc_ref,
):
    @pl.when(pl.program_id(0) == 0)
    def _():
        acc_ref[...] = dsum_ref[...]

    d_ffn = dffn_ref[...]
    d_own = (nt(d_ffn, wdo_ref[...]) * so_ref[...].astype(F32)).astype(BF)
    d_other = (nn(d_ffn, wdx_ref[...]) * sx_ref[...].astype(F32)).astype(BF)
    duo_ref[...] = d_own
    bup_ref[...] = jnp.broadcast_to(down_sum(d_own.astype(F32)), bup_ref.shape)
    acc_ref[...] += nt(d_own, wuo_ref[...]) + nt(d_other, wux_ref[...])

    @pl.when(pl.program_id(0) == pl.num_programs(0) - 1)
    def _():
        d_normed = acc_ref[...]
        n, inverse = moments(hid_ref[...])
        d_hidden = norm_backward(d_normed, n, inverse, g_ref[...])
        d_attn = d_hidden.astype(BF)
        dhid_ref[...] = d_hidden
        dattn_ref[...] = d_attn
        dctx_ref[...] = nt(d_attn, wpo_ref[...]).astype(BF)
        stats_ref[...] = jnp.zeros_like(stats_ref)
        stats_ref[0:1] = down_sum(d_normed * n)
        stats_ref[1:2] = down_sum(d_normed)
        stats_ref[2:3] = down_sum(d_attn.astype(F32))


def input_total(parts, dhid_ref, *refs):
    at = 0
    for mine_ref, theirs_ref in zip(refs[:parts], refs[parts:2 * parts]):
        rows = pl.ds(at, mine_ref.shape[0])
        refs[-1][rows, :] = dhid_ref[rows, :] + (mine_ref[...] + theirs_ref[...])
        at += mine_ref.shape[0]


def put(g, core_ref, outs, rows, order, extra=None):
    if len(outs) == 1:
        outs[0][:g.shape[0]] = g
        if extra is not None:
            outs[0][g.shape[0]:] = extra
        return
    keep_ref, send_ref = outs
    first = core_ref[0] == 0
    for block in range(8):
        at = 2 * block * rows
        even, odd = g[at:at + rows], g[at + rows:at + 2 * rows]
        bits = {"u": block // 4, "l": block // 2 % 2, "x": block % 2}
        place = tuple(bits[stage] for stage in order)
        keep_ref[place + (slice(0, rows),)] = jnp.where(first, even, odd)
        send_ref[place + (slice(0, rows),)] = jnp.where(first, odd, even)
        if extra is not None:
            keep_ref[place + (slice(rows, None),)] = extra
            send_ref[place + (slice(rows, None),)] = extra


def turn(refs, turned, step=0):
    @pl.when(pl.program_id(0) == step)
    def _():
        at = 0
        for ref in refs:
            turned[:, at:at + ref.shape[0]] = ref[...].T
            at += ref.shape[0]


def gradient(left_ref, right_ref, out_ref, turned):
    turn((left_ref,), turned)
    out_ref[...] = nn(turned[...], right_ref[...])


def gradient_up(rows, core_ref, la_ref, lb_ref, right_ref, proj_ref, ca_ref, cb_ref, *rest):
    turned, outs = rest[-1], rest[:-1]
    last = pl.num_programs(0) - 1
    count = len(outs) // 2
    length = la_ref.shape[0]
    turn((la_ref, lb_ref), turned)
    turn((proj_ref,), turned, last)

    @pl.when(pl.program_id(0) < last // 2)
    def _():
        put(nn(turned[...], right_ref[...]), core_ref, outs[:count], rows, UP_ORDERS[0])

    @pl.when((pl.program_id(0) >= last // 2) & (pl.program_id(0) < last))
    def _():
        put(nn(turned[...], right_ref[...]), core_ref, outs[count:], rows, UP_ORDERS[1])

    @pl.when(pl.program_id(0) == last)
    def _():
        g = nn(turned[:, :length], ca_ref[...]) + nn(turned[:, length:], cb_ref[...])
        put(g, core_ref, outs[count:], rows, UP_ORDERS[1])


def gradient_attention(
    rows, core_ref, x_ref, dqkv_ref, f_ref, a_ref, up_ref, ka_ref, kb_ref, *rest
):
    turned, outs = rest[-1], rest[:-1]
    count = len(outs) // 2
    width = x_ref.shape[1]
    half = width // 2
    up, qkv = up_ref[...], ka_ref[...] + kb_ref[...]
    pieces = [f_ref[:3], a_ref[:3]] + [
        up[:1, at * width:(at + 1) * width] for at in range(up.shape[1] // width)
    ] + [jnp.concatenate([qkv[:1, :half], qkv[:1, 2 * half:]], axis=1)]
    have = sum(piece.shape[0] for piece in pieces)
    pieces.append(jnp.zeros((-have % 16, width), F32))
    extra = jnp.concatenate(pieces, axis=0)
    turn((x_ref,), turned)
    put(nn(turned[...], dqkv_ref[:, :2 * half]), core_ref, outs[:count], rows, LAST_ORDERS[0], extra)
    put(nn(turned[...], dqkv_ref[:, 2 * half:]), core_ref, outs[count:], rows, LAST_ORDERS[1])


def join_pieces(place_ref, *refs):
    out_ref = refs[-1]
    rows = refs[0].shape[0]
    for mine in (True, False):
        base = (place_ref[0] if mine else 1 - place_ref[0]) * 4
        pieces = refs[:5] if mine else refs[5:10]
        starts = [base + jnp.bitwise_xor(place_ref[1], piece) for piece in (0, 1, 2, 3, 3)]
        for index, (at, piece) in enumerate(zip(starts, pieces)):
            start = at * rows + (rows // 2 if index == 4 else 0)
            out_ref[pl.ds(pl.multiple_of(start, 16), piece.shape[0])] = piece[...].astype(BF)


def pick(array, index, axis):
    return lax.dynamic_index_in_dim(array, index, axis, keepdims=False)


def lock(*values):
    return lax.optimization_barrier(values)


def on_device(
    dp, inputs, segment_ids, pad_flags, w_query, w_key, w_value, b_query, b_value, w_proj, b_proj,
    gain_attn, shift_attn, w_up, b_up, w_down, b_down, gain_ffn, shift_ffn, cotangent,
):
    d = lax.axis_index("dp")
    tokens, width = inputs.shape
    half = w_query.shape[1]
    units = w_up.shape[1]
    core, low = d % 2, (d // 2) % 4
    pair = range(tokens // LENGTH)

    def swap_mp(array):
        return lax.ppermute(array, "mp", [(0, 1), (1, 0)])

    def swap_dp(array, bit):
        return lax.ppermute(array, "dp", [(i, i ^ bit) for i in range(dp)])

    def row(vector):
        return vector.reshape(1, -1)

    full = lambda array: (array, None, None)

    rows = width // 8
    place_d = jnp.stack([core, low]).astype(jnp.int32)

    def eighth(weight):
        return lax.dynamic_slice_in_dim(weight, (core * 4 + low) * rows, rows, 0).astype(F32)

    def eighth_t(weight):
        return lax.dynamic_slice_in_dim(weight, (core * 4 + low) * rows, rows, 1).T.astype(F32)

    def near_pieces(own):
        return swap_dp(own, 2), swap_dp(own, 4)

    def far_pieces(by_x, by_z):
        return swap_dp(by_z[:rows // 2], 2), swap_dp(by_x[rows // 2:], 4)

    def join(mine, theirs):
        (joined,) = call(
            join_pieces, (1,), [(place_d, "smem", None)] + [full(a) for a in mine + theirs],
            [((width, mine[0].shape[1]), BF, None, None)],
            micros=3.0,
        )
        return joined

    def other_core(pieces):
        return tuple(swap_dp(piece, 1) for piece in pieces)

    def tokens_of(array, at):
        return lax.slice_in_dim(array, at * LENGTH, (at + 1) * LENGTH, axis=0)

    def sequence(array, at):
        return (array, (LENGTH, array.shape[1]), lambda *_: (at, 0))

    square = pltpu.VMEM((LENGTH, LENGTH), F32)
    heads = half // HD
    lanes = (LENGTH, half)
    masks = []
    for at in pair:
        seg, pad = tokens_of(segment_ids, at), tokens_of(pad_flags, at)
        masks.append([full(seg.reshape(-1, 1)), full(row(seg)), full(pad.reshape(-1, 1))])
    own_qkv = [full(w_query), full(w_key), full(w_value)]

    def attend(at, token):
        return call(
            attend_forward, (1,),
            [sequence(token, at)] + own_qkv + [full(row(b_query)), full(row(b_value)), full(row(b_up))]
            + masks[at],
            [(lanes, BF, None, None)] * 4
            + [((LENGTH + 8 * (at == 0), half), F32, None, None), ((heads, LENGTH), F32, None, None)],
            [square], micros=9.0,
        )

    shard = width // dp
    (proj,) = lock(swap_mp(eighth_t(w_proj)))
    down_y = swap_mp(lax.dynamic_slice_in_dim(w_down, d * shard, shard, 1).T.astype(F32))
    saved = [attend(0, lock(inputs, proj)[0])]
    proj, proj_near, up, down_y, saved[0] = lock(
        proj, near_pieces(proj), swap_mp(lock(eighth(w_up), proj)[0]), down_y, tuple(saved[0])
    )
    down_oth = lax.all_gather(down_y, "dp", axis=0, tiled=True)
    saved.append(attend(1, lock(inputs, proj)[0]))
    proj = (proj,) + tuple(proj_near)
    proj_far = far_pieces(*proj_near)
    ctx_a, up_near, proj_far, proj_core, saved[1] = lock(
        swap_mp(saved[0][4]), near_pieces(up), proj_far, other_core(proj), tuple(saved[1])
    )
    proj_far, proj_far_core, proj, proj_core = lock(
        proj_far, other_core(proj_far), proj, proj_core
    )

    steps = units // UNIT_BLOCK
    unit_row = lambda array: (array, (1, UNIT_BLOCK), lambda i: (0, i))
    unit_col = lambda array: (array, (array.shape[0], UNIT_BLOCK), lambda i: (0, i))
    unit_block = lambda array: (array, (UNIT_BLOCK, width), lambda i: (i, 0))
    unit_all = lambda array, block: (array, (array.shape[0], block), lambda i: (0, i))
    column = lambda array: (array, (array.shape[0], half), lambda i: (0, i))
    token = lambda dtype: ((LENGTH, width), dtype, None, None)
    stat = ((8, width), F32, None, None)
    def rows_of(at, cols, dtype, block=None):
        if block is None:
            return ((tokens, cols), dtype, (LENGTH, cols), lambda *_: (at, 0))
        return ((tokens, cols), dtype, (LENGTH, block), lambda i: (at, i))

    proj_oth = join(proj + tuple(proj_far), proj_core + tuple(proj_far_core))

    def forward_own(at, context, before):
        outs = call(
            feed_own, (steps,),
            [sequence(inputs, at), full(saved[at][3]), full(context), full(w_proj), full(proj_oth),
             full(row(b_proj)), full(row(gain_attn)), full(row(shift_attn)), full(row(b_down)),
             unit_col(w_up), unit_row(row(b_up)), unit_block(w_down)]
            + [(array, "any", None) for array in before],
            [token(BF), token(F32), rows_of(at, width, F32), rows_of(at, units, BF, UNIT_BLOCK),
             rows_of(at, units, BF, UNIT_BLOCK)],
            micros=8.0, alias={12 + i: 2 + i for i in range(len(before))},
        )
        return outs[0], outs[1], outs[2:]

    def forward_other(at, normed, before):
        return call(
            feed_up, (units // half,),
            [full(normed), column(joined), (ctx_a, (8, half), lambda i: (LENGTH // 8, 0))]
            + [(array, "any", None) for array in before],
            [rows_of(at, units, BF, half)] * 2, micros=4.0,
            alias={3 + i: i for i in range(len(before))},
        )

    normed_a, partial_a, kept = forward_own(0, ctx_a, ())
    up = (up,) + tuple(up_near)
    ctx_b, up_far, up_core, normed_a, partial_a, kept = lock(
        swap_mp(saved[1][4]), far_pieces(*up_near), other_core(up), normed_a, partial_a, tuple(kept)
    )
    up, up_far, up_far_core, up_core, normed_a, ctx_b = lock(
        up, up_far, other_core(up_far), up_core, normed_a, ctx_b
    )
    joined = join(up + tuple(up_far), up_core + tuple(up_far_core))
    other = forward_other(0, normed_a, ())
    normed_b, partial_b, (hidden, act_own, slope_own) = forward_own(1, ctx_b, kept)
    act_oth, slope_oth = forward_other(1, normed_b, other)
    every = lambda dtype: ((tokens, width), dtype, None, None)
    outputs, d_summed, d_ffn, stats_ffn, down_oth = call(
        feed_down, (1,),
        [full(act_oth), full(partial_a), full(partial_b), full(down_oth), full(row(gain_ffn)),
         full(row(shift_ffn)), full(cotangent)],
        [every(BF), every(F32), every(BF), stat, ((width, units), BF, None, None)], micros=10.0,
    )

    split = dp == 16
    core_arg = jnp.reshape(core, (1,)).astype(jnp.int32)
    lead = (2, 2, 2, width // dp)
    turned = pltpu.VMEM((width, tokens), BF)

    def parted(cols, block, index, extra=0):
        if not split:
            out = ((width + extra, cols), F32, (width + extra, block), lambda i: (0, index(i)))
            return [out]
        shape = lead[:-1] + (lead[-1] + extra,)
        return [(shape + (cols,), F32, shape + (block,), lambda i: (0, 0, 0, 0, index(i)))] * 2

    def pairs(outs):
        return outs[:len(outs) // 2], outs[len(outs) // 2:]

    bits = {"x": (d // 2) % 2, "l": (d // 4) % 2, "u": d // 8}
    hops = {"x": 2, "l": 4, "u": 8}

    class Reduction:
        def __init__(self, parts, order, terms=None):
            self.order, self.parts, self.terms = list(order), parts, terms

        def step(self):
            if not split:
                return self.parts[0]
            if self.terms is None:
                got = swap_dp(self.parts[1], 1)
                self.terms = [self.parts[0], got]
                return got
            stage = self.order.pop(0)
            bit = bits[stage]
            send = sum(pick(term, 1 - bit, 0) for term in self.terms)
            got = swap_dp(send, hops[stage])
            self.terms = [pick(term, bit, 0) for term in self.terms] + [got]
            return got

        def result(self):
            if not split:
                return lax.psum_scatter(self.parts[0], "dp", scatter_dimension=0, tiled=True)
            while self.order:
                self.step()
            return sum(self.terms)

    (down_whole,) = call(
        gradient, (units // UNIT_BLOCK,), [full(d_ffn), unit_all(act_own, UNIT_BLOCK)],
        [((width, units), F32, (width, UNIT_BLOCK), lambda i: (0, i))], [turned], 6.0,
    )
    d_ffn, down_whole = lock(d_ffn, down_whole)
    down_part = lax.psum_scatter(down_whole, "dp", scatter_dimension=0, tiled=True)
    back = lambda array: (array, (array.shape[0], BACK_BLOCK), lambda i: (0, i))
    d_up, sums_up, d_hidden, d_attn, d_context, stats_attn = call(
        feed_backward, (units // BACK_BLOCK,),
        [full(d_ffn), back(slope_own), back(slope_oth),
         (w_down, (BACK_BLOCK, width), lambda i: (i, 0)), back(down_oth), back(w_up), back(joined),
         full(d_summed), full(hidden), full(row(gain_attn)), full(w_proj)],
        [((tokens, units), BF, (tokens, BACK_BLOCK), lambda i: (0, i)),
         ((8, units), F32, (8, BACK_BLOCK), lambda i: (0, i)), every(F32), every(BF),
         ((tokens, half), BF, None, None), stat],
        [pltpu.VMEM((tokens, width), F32)], micros=20.0,
    )

    def back_attend(at, grad, before, sizes):
        q, k, v, _, _, lse = saved[at]
        outs = call(
            functools.partial(attend_backward, len(sizes)), (1,),
            [full(q), full(k), full(v), full(lse), sequence(grad, at)] + masks[at] + own_qkv
            + [(array, "any", None) for array in before],
            [rows_of(at, 3 * half, BF), ((8, 3 * half), F32, None, None)]
            + [((size, width), F32, None, None) for size in sizes],
            [square], micros=9.0, alias={11: 0} if before else {},
        )
        return outs[0], outs[1], list(outs[2:])

    blocks = units // half
    up = call(
        functools.partial(gradient_up, lead[-1]), (blocks + 1,),
        [(core_arg, "smem", None), full(normed_a), full(normed_b),
         (d_up, (tokens, half), lambda i: (0, jnp.minimum(i, blocks - 1))), full(d_attn),
         full(saved[0][3]), full(saved[1][3])],
        parted(units // 2, half, lambda i: jnp.minimum(i, blocks // 2 - 1))
        + parted(units // 2 + half, half, lambda i: jnp.maximum(i - blocks // 2, 0)),
        [turned], 9.0,
    )
    up, d_context = lock(up, d_context)
    up = [Reduction(parts, order) for parts, order in zip(pairs(up), UP_ORDERS)]

    def advance(reductions, *values):
        for one in reductions:
            one.step()
        if not split:
            return lock(*values)
        terms, *values = lock([one.terms for one in reductions], *values)
        for one, changed in zip(reductions, terms):
            one.terms = list(changed)
        return values

    dqkv, sums_a, mine_a = back_attend(0, d_context, (), (256, 256))
    dqkv, mine_a, d_context = advance(up, dqkv, mine_a, d_context)
    theirs_a = [swap_mp(mine_a[0])]
    dqkv, sums_b, mine_b = back_attend(1, d_context, (dqkv,), (128, 256, 128))
    dqkv, mine_a, mine_b, theirs_a = advance(up, dqkv, mine_a, mine_b, theirs_a)
    theirs_a.append(swap_mp(mine_a[1]))
    last = call(
        functools.partial(gradient_attention, lead[-1]), (1,),
        [(core_arg, "smem", None), full(inputs), full(dqkv)]
        + [full(a) for a in (stats_ffn, stats_attn, sums_up, sums_a, sums_b)],
        parted(2 * half, 2 * half, lambda i: 0, 16) + parted(half, half, lambda i: 0),
        [turned], 7.0,
    )
    last, mine_b, theirs_a, down_part = advance(up, last, mine_b, theirs_a, down_part)
    query, value = [Reduction(parts, order) for parts, order in zip(pairs(last), LAST_ORDERS)]
    theirs_b = []
    for moving in (up + [query, value], [query, value], [query, value]):
        theirs_b.append(swap_mp(mine_b[len(theirs_b)]))
        mine_b, theirs_b = advance(moving, mine_b, theirs_b)
    if split:
        query_part, value_part = query.result(), value.result()
        vectors = query_part[shard:]
    else:
        (whole,) = query.parts
        vectors = lax.psum(whole[width:], "dp")
        query_part = lax.psum_scatter(whole[:width], "dp", scatter_dimension=0, tiled=True)
        value_part = value.result()
    query_part = query_part[:shard]
    up_part = [one.result() for one in up]
    proj_part = up_part[1][:, units // 2:]
    up_part = jnp.concatenate([up_part[0], up_part[1][:, :units // 2]], axis=1)

    grad_inputs = None
    for at, (mine, theirs) in enumerate(((mine_a, theirs_a), (mine_b, theirs_b))):
        ins = [sequence(d_hidden, at)] + [full(a) for a in list(mine) + list(theirs)]
        before = len(ins)
        if grad_inputs is not None:
            ins.append((grad_inputs, "any", None))
        (grad_inputs,) = call(
            functools.partial(input_total, len(mine)), (1,), ins, [rows_of(at, width, F32)],
            micros=2.5, alias={} if at == 0 else {before: 0},
        )
    return (
        outputs,
        grad_inputs,
        query_part[:, :half],
        query_part[:, half:],
        value_part,
        vectors[8, :half],
        vectors[8, half:],
        proj_part.T,
        vectors[5],
        vectors[3],
        vectors[4],
        up_part,
        vectors[6:8].reshape(-1),
        down_part.T,
        vectors[2],
        vectors[0],
        vectors[1],
    )


def solution(mesh):
    placed = (
        P("dp", None), P("dp"), P("dp"), P(None, "mp"), P(None, "mp"), P(None, "mp"), P("mp"),
        P("mp"), P("mp", None), P(), P(), P(), P(None, "mp"), P("mp"), P("mp", None), P(), P(), P(),
        P("dp", None),
    )
    return jax.shard_map(
        functools.partial(on_device, mesh.shape["dp"]),
        mesh=mesh,
        in_specs=placed,
        out_specs=(
            P("dp", None), P("dp", None), P("dp", "mp"), P("dp", "mp"), P("dp", "mp"), P("mp"),
            P("mp"), P("mp", "dp"), P(), P(), P(), P("dp", "mp"), P("mp"), P("mp", "dp"), P(), P(),
            P(),
        ),
        check_vma=False,
    )
```

```python
import functools
import math

import jax
import jax.numpy as jnp
from jax import lax
from jax.experimental import pallas as pl
from jax.experimental.pallas import tpu as pltpu
from jax.sharding import PartitionSpec as P

HD = 64
LENGTH = 512
QUERY_CHUNK = 256
UNIT_BLOCK = 512
BACK_BLOCK = 256
UP_ORDERS = ("lux", "xlu")
LAST_ORDERS = ("xlu", "lux")
norm_eps = 1e-05
masked_value = -1000000000.0
BF = jnp.bfloat16
F32 = jnp.float32
VMEM_BYTES = 50 * 1024 * 1024


def nn(a, b):
    return lax.dot_general(a, b, (((1,), (0,)), ((), ())), preferred_element_type=F32)


def nt(a, b):
    return lax.dot_general(a, b, (((1,), (1,)), ((), ())), preferred_element_type=F32)


def call(body, grid, ins, outs, scratch=(), micros=1.0, alias=None):
    def spec(shape, block, index):
        if block == "smem":
            return pl.BlockSpec(memory_space=pltpu.SMEM)
        if block == "any":
            return pl.BlockSpec(memory_space=pl.ANY)
        if block is None:
            return pl.BlockSpec(shape, lambda *_: (0,) * len(shape))
        return pl.BlockSpec(block, index)

    moved = sum(a.size * a.dtype.itemsize for a, _, _ in ins)
    moved += sum(math.prod(s) * jnp.dtype(d).itemsize for s, d, _, _ in outs)
    return pl.pallas_call(
        body,
        grid=grid,
        in_specs=[spec(a.shape, b, i) for a, b, i in ins],
        out_specs=[spec(s, b, i) for s, _, b, i in outs],
        out_shape=[jax.ShapeDtypeStruct(s, d) for s, d, _, _ in outs],
        scratch_shapes=list(scratch),
        input_output_aliases=alias or {},
        compiler_params=pltpu.CompilerParams(vmem_limit_bytes=VMEM_BYTES),
        cost_estimate=pl.CostEstimate(
            flops=int(micros * 1.15e9), bytes_accessed=moved, transcendentals=0
        ),
    )(*[a for a, _, _ in ins])


def mask_bias(segc_ref, segr_ref, padc_ref, bias_ref):
    shape = bias_ref.shape
    key = lax.broadcasted_iota(jnp.int32, shape, 0)
    query = lax.broadcasted_iota(jnp.int32, shape, 1)
    same = segc_ref[...] == segr_ref[...]
    allowed = same & ((padc_ref[...] == 0) | (key == query))
    bias_ref[...] = jnp.where(allowed, 0.0, masked_value)


def attend_forward(
    x_ref, wq_ref, wk_ref, wv_ref, bq_ref, bv_ref, bu_ref, segc_ref, segr_ref, padc_ref,
    q_ref, k_ref, v_ref, ctx_ref, send_ref, lse_ref, bias_ref,
):
    x = x_ref[...]
    q_ref[...] = ((nn(x, wq_ref[...]) + bq_ref[...]).astype(BF).astype(F32) * HD ** (-0.5)).astype(BF)
    k_ref[...] = nn(x, wk_ref[...]).astype(BF)
    v_ref[...] = (nn(x, wv_ref[...]) + bv_ref[...]).astype(BF)
    mask_bias(segc_ref, segr_ref, padc_ref, bias_ref)
    length, wide = x.shape[0], q_ref.shape[1]
    if send_ref.shape[0] > length:
        send_ref[length:] = jnp.zeros((send_ref.shape[0] - length, wide), F32)
        for at in range(bu_ref.shape[1] // wide):
            send_ref[length + at:length + at + 1] = bu_ref[:, at * wide:(at + 1) * wide]

    def pair(index, carry):
        cols = pl.ds(pl.multiple_of(index * 128, 128), 128)
        keys = k_ref[:, cols]
        values_t = v_ref[:, cols].T
        lane = lax.broadcasted_iota(jnp.int32, (QUERY_CHUNK, 128), 1)
        for start in range(0, length, QUERY_CHUNK):
            rows = pl.ds(start, QUERY_CHUNK)
            query = q_ref[rows, cols]
            parts = []
            for head in range(2):
                one = jnp.where((lane < HD) == (head == 0), query, jnp.zeros_like(query))
                scores = nt(keys, one) + bias_ref[:, rows]
                highest = jnp.max(scores, axis=0, keepdims=True)
                grown = jnp.exp(scores - highest)
                total = jnp.sum(grown, axis=0, keepdims=True)
                weights = (grown * (1.0 / total)).astype(BF)
                lse_ref[pl.ds(2 * index + head, 1), rows] = highest + jnp.log(total)
                parts.append(nn(values_t[head * HD:(head + 1) * HD], weights))
            context = jnp.concatenate(parts, axis=0).T.astype(BF)
            ctx_ref[rows, cols] = context
            send_ref[rows, cols] = context.astype(F32)
        return carry

    lax.fori_loop(0, q_ref.shape[1] // 128, pair, 0)


def attend_backward(
    parts, q_ref, k_ref, v_ref, lse_ref, dctx_ref, segc_ref, segr_ref, padc_ref, wq_ref, wk_ref, wv_ref, *rest
):
    bias_ref, part_refs = rest[-1], rest[-1 - parts:-1]
    dqkv_ref, sums_ref = rest[-3 - parts:-1 - parts]
    mask_bias(segc_ref, segr_ref, padc_ref, bias_ref)
    length, width = q_ref.shape

    def pair(index, carry):
        first = pl.multiple_of(index * 128, 128)
        cols = pl.ds(first, 128)
        keys = k_ref[:, cols]
        values = v_ref[:, cols]
        keys_t = keys.T
        lane = lax.broadcasted_iota(jnp.int32, (QUERY_CHUNK, 128), 1)
        d_keys = [None, None]
        d_values = [None, None]
        for start in range(0, length, QUERY_CHUNK):
            rows = pl.ds(start, QUERY_CHUNK)
            query = q_ref[rows, cols]
            grad = dctx_ref[rows, cols]
            d_query = []
            for head in range(2):
                here = (lane < HD) == (head == 0)
                scores = nt(keys, jnp.where(here, query, jnp.zeros_like(query))) + bias_ref[:, rows]
                prob = jnp.exp(scores - lse_ref[pl.ds(2 * index + head, 1), rows])
                weights = prob.astype(BF)
                d_prob = nt(values, jnp.where(here, grad, jnp.zeros_like(grad)))
                inner = jnp.sum(prob * d_prob, axis=0, keepdims=True)
                raw = (prob * (d_prob - inner)).astype(BF)
                dv = nn(weights, grad)
                dk = nn(raw, query)
                d_values[head] = dv if start == 0 else d_values[head] + dv
                d_keys[head] = dk if start == 0 else d_keys[head] + dk
                d_query.append(nn(keys_t[head * HD:(head + 1) * HD], raw))
            dq = (jnp.concatenate(d_query, axis=0).T * HD ** (-0.5)).astype(BF)
            dqkv_ref[rows, cols] = dq
        full = lax.broadcasted_iota(jnp.int32, (length, 128), 1) < HD
        dqkv_ref[:, pl.ds(pl.multiple_of(width + first, 128), 128)] = jnp.where(
            full, d_keys[0], d_keys[1]
        ).astype(BF)
        dqkv_ref[:, pl.ds(pl.multiple_of(2 * width + first, 128), 128)] = jnp.where(
            full, d_values[0], d_values[1]
        ).astype(BF)
        return carry

    lax.fori_loop(0, width // 128, pair, 0)
    sums_ref[...] = jnp.broadcast_to(
        jnp.sum(dqkv_ref[...].astype(F32), axis=0, keepdims=True), sums_ref.shape
    )
    total = None
    for part, weight in enumerate((wq_ref, wk_ref, wv_ref)):
        term = nt(dqkv_ref[:, part * width:(part + 1) * width], weight[...])
        total = term if total is None else total + term
    at = 0
    for part_ref in part_refs:
        part_ref[...] = total[at:at + part_ref.shape[0]]
        at += part_ref.shape[0]


def moments(values):
    average = jnp.mean(values, axis=-1, keepdims=True)
    centered = values - average
    variance = jnp.mean(centered * centered, axis=-1, keepdims=True)
    inverse = lax.rsqrt(variance + norm_eps)
    return centered * inverse, inverse


def norm_backward(upstream, n, inverse, gain):
    scaled = upstream * gain
    return inverse * (
        scaled
        - jnp.mean(scaled, axis=-1, keepdims=True)
        - n * jnp.mean(scaled * n, axis=-1, keepdims=True)
    )


def down_sum(values):
    return jnp.sum(values, axis=0, keepdims=True)


def activate(nlow, wu_ref, bias, act_ref, slope_ref):
    up = nn(nlow, wu_ref[...]) + bias
    cdf = 0.5 * (1.0 + lax.erf(up * 2.0 ** (-0.5)))
    active = (up * cdf).astype(BF)
    act_ref[...] = active
    slope = cdf + up * jnp.exp(-0.5 * up * up) * (1.0 / math.sqrt(2.0 * math.pi))
    slope_ref[...] = slope.astype(BF)
    return active


def feed_own(
    x_ref, co_ref, cx_ref, wpo_ref, wpx_ref, bp_ref, g_ref, s_ref, bd_ref, wu_ref, bu_ref, wd_ref, *rest
):
    nlow_ref, acc_ref, hid_ref, act_ref, slope_ref = rest[-5:]

    @pl.when(pl.program_id(0) == 0)
    def _():
        attn = nn(co_ref[...], wpo_ref[...]) + nt(cx_ref[:x_ref.shape[0]].astype(BF), wpx_ref[...]) + bp_ref[...]
        hidden = x_ref[...].astype(F32) + attn
        hid_ref[...] = hidden
        n, _ = moments(hidden)
        normed = n * g_ref[...] + s_ref[...]
        nlow_ref[...] = normed.astype(BF)
        acc_ref[...] = normed + bd_ref[...]

    acc_ref[...] += nn(activate(nlow_ref[...], wu_ref, bu_ref[...], act_ref, slope_ref), wd_ref[...])


def feed_up(nlow_ref, wu_ref, bu_ref, *rest):
    bias = bu_ref[pl.ds(pl.program_id(0), 1), :]
    activate(nlow_ref[...], wu_ref, bias, *rest[-2:])


def feed_down(
    act_ref, starta_ref, startb_ref, wd_ref, g_ref, s_ref, cot_ref,
    out_ref, dsum_ref, dffn_ref, stats_ref, low_ref,
):
    weights = wd_ref[...].astype(BF)
    low_ref[...] = weights
    stats_ref[...] = jnp.zeros_like(stats_ref)
    length = starta_ref.shape[0]
    for at, start_ref in enumerate((starta_ref, startb_ref)):
        rows = pl.ds(at * length, length)
        total = start_ref[...] + nt(act_ref[rows, :], weights)
        n, inverse = moments(total)
        out_ref[rows, :] = (n * g_ref[...] + s_ref[...]).astype(BF)
        cot = cot_ref[rows, :].astype(F32)
        d_summed = norm_backward(cot, n, inverse, g_ref[...])
        d_ffn = d_summed.astype(BF)
        dsum_ref[rows, :] = d_summed
        dffn_ref[rows, :] = d_ffn
        stats_ref[0:1] += down_sum(cot * n)
        stats_ref[1:2] += down_sum(cot)
        stats_ref[2:3] += down_sum(d_ffn.astype(F32))


def feed_backward(
    dffn_ref, so_ref, sx_ref, wdo_ref, wdx_ref, wuo_ref, wux_ref, dsum_ref, hid_ref, g_ref, wpo_ref,
    duo_ref, bup_ref, dhid_ref, dattn_ref, dctx_ref, stats_ref, acc_ref,
):
    @pl.when(pl.program_id(0) == 0)
    def _():
        acc_ref[...] = dsum_ref[...]

    d_ffn = dffn_ref[...]
    d_own = (nt(d_ffn, wdo_ref[...]) * so_ref[...].astype(F32)).astype(BF)
    d_other = (nn(d_ffn, wdx_ref[...]) * sx_ref[...].astype(F32)).astype(BF)
    duo_ref[...] = d_own
    bup_ref[...] = jnp.broadcast_to(down_sum(d_own.astype(F32)), bup_ref.shape)
    acc_ref[...] += nt(d_own, wuo_ref[...]) + nt(d_other, wux_ref[...])

    @pl.when(pl.program_id(0) == pl.num_programs(0) - 1)
    def _():
        d_normed = acc_ref[...]
        n, inverse = moments(hid_ref[...])
        d_hidden = norm_backward(d_normed, n, inverse, g_ref[...])
        d_attn = d_hidden.astype(BF)
        dhid_ref[...] = d_hidden
        dattn_ref[...] = d_attn
        dctx_ref[...] = nt(d_attn, wpo_ref[...]).astype(BF)
        stats_ref[...] = jnp.zeros_like(stats_ref)
        stats_ref[0:1] = down_sum(d_normed * n)
        stats_ref[1:2] = down_sum(d_normed)
        stats_ref[2:3] = down_sum(d_attn.astype(F32))


def input_total(parts, dhid_ref, *refs):
    at = 0
    for mine_ref, theirs_ref in zip(refs[:parts], refs[parts:2 * parts]):
        rows = pl.ds(at, mine_ref.shape[0])
        refs[-1][rows, :] = dhid_ref[rows, :] + (mine_ref[...] + theirs_ref[...])
        at += mine_ref.shape[0]


def put(g, core_ref, outs, rows, order, extra=None):
    if len(outs) == 1:
        outs[0][:g.shape[0]] = g
        if extra is not None:
            outs[0][g.shape[0]:] = extra
        return
    keep_ref, send_ref = outs
    first = core_ref[0] == 0
    for block in range(8):
        at = 2 * block * rows
        even, odd = g[at:at + rows], g[at + rows:at + 2 * rows]
        bits = {"u": block // 4, "l": block // 2 % 2, "x": block % 2}
        place = tuple(bits[stage] for stage in order)
        keep_ref[place + (slice(0, rows),)] = jnp.where(first, even, odd)
        send_ref[place + (slice(0, rows),)] = jnp.where(first, odd, even)
        if extra is not None:
            keep_ref[place + (slice(rows, None),)] = extra
            send_ref[place + (slice(rows, None),)] = extra


def turn(refs, turned, step=0):
    @pl.when(pl.program_id(0) == step)
    def _():
        at = 0
        for ref in refs:
            turned[:, at:at + ref.shape[0]] = ref[...].T
            at += ref.shape[0]


def gradient(left_ref, right_ref, out_ref, turned):
    turn((left_ref,), turned)
    out_ref[...] = nn(turned[...], right_ref[...])


def gradient_up(rows, core_ref, la_ref, lb_ref, right_ref, proj_ref, ca_ref, cb_ref, *rest):
    turned, outs = rest[-1], rest[:-1]
    last = pl.num_programs(0) - 1
    count = len(outs) // 2
    length = la_ref.shape[0]
    turn((la_ref, lb_ref), turned)
    turn((proj_ref,), turned, last)

    @pl.when(pl.program_id(0) < last // 2)
    def _():
        put(nn(turned[...], right_ref[...]), core_ref, outs[:count], rows, UP_ORDERS[0])

    @pl.when((pl.program_id(0) >= last // 2) & (pl.program_id(0) < last))
    def _():
        put(nn(turned[...], right_ref[...]), core_ref, outs[count:], rows, UP_ORDERS[1])

    @pl.when(pl.program_id(0) == last)
    def _():
        g = nn(turned[:, :length], ca_ref[...]) + nn(turned[:, length:], cb_ref[...])
        put(g, core_ref, outs[count:], rows, UP_ORDERS[1])


def gradient_attention(
    rows, core_ref, x_ref, dqkv_ref, f_ref, a_ref, up_ref, ka_ref, kb_ref, *rest
):
    turned, outs = rest[-1], rest[:-1]
    count = len(outs) // 2
    width = x_ref.shape[1]
    half = width // 2
    up, qkv = up_ref[...], ka_ref[...] + kb_ref[...]
    pieces = [f_ref[:3], a_ref[:3]] + [
        up[:1, at * width:(at + 1) * width] for at in range(up.shape[1] // width)
    ]
    extra = jnp.concatenate(pieces, axis=0)
    biases = jnp.concatenate([qkv[:1, :half], qkv[:1, 2 * half:], jnp.zeros((6, half), F32)], axis=0)
    turn((x_ref,), turned)
    put(nn(turned[...], dqkv_ref[:, :2 * half]), core_ref, outs[:count], rows, LAST_ORDERS[0], extra)
    put(nn(turned[...], dqkv_ref[:, 2 * half:]), core_ref, outs[count:], rows, LAST_ORDERS[1], biases)


def join_pieces(place_ref, *refs):
    out_ref = refs[-1]
    rows = refs[0].shape[0]
    for mine in (True, False):
        base = (place_ref[0] if mine else 1 - place_ref[0]) * 4
        pieces = refs[:5] if mine else refs[5:10]
        starts = [base + jnp.bitwise_xor(place_ref[1], piece) for piece in (0, 1, 2, 3, 3)]
        for index, (at, piece) in enumerate(zip(starts, pieces)):
            start = at * rows + (rows // 2 if index == 4 else 0)
            out_ref[pl.ds(pl.multiple_of(start, 16), piece.shape[0])] = piece[...].astype(BF)


def pick(array, index, axis):
    return lax.dynamic_index_in_dim(array, index, axis, keepdims=False)


def lock(*values):
    return lax.optimization_barrier(values)


def on_device(
    dp, inputs, segment_ids, pad_flags, w_query, w_key, w_value, b_query, b_value, w_proj, b_proj,
    gain_attn, shift_attn, w_up, b_up, w_down, b_down, gain_ffn, shift_ffn, cotangent,
):
    d = lax.axis_index("dp")
    tokens, width = inputs.shape
    half = w_query.shape[1]
    units = w_up.shape[1]
    core, low = d % 2, (d // 2) % 4
    pair = range(tokens // LENGTH)

    def swap_mp(array):
        return lax.ppermute(array, "mp", [(0, 1), (1, 0)])

    def swap_dp(array, bit):
        return lax.ppermute(array, "dp", [(i, i ^ bit) for i in range(dp)])

    def row(vector):
        return vector.reshape(1, -1)

    full = lambda array: (array, None, None)

    rows = width // 8
    place_d = jnp.stack([core, low]).astype(jnp.int32)

    def eighth(weight):
        return lax.dynamic_slice_in_dim(weight, (core * 4 + low) * rows, rows, 0).astype(F32)

    def eighth_t(weight):
        return lax.dynamic_slice_in_dim(weight, (core * 4 + low) * rows, rows, 1).T.astype(F32)

    def near_pieces(own):
        return swap_dp(own, 2), swap_dp(own, 4)

    def far_pieces(by_x, by_z):
        return swap_dp(by_z[:rows // 2], 2), swap_dp(by_x[rows // 2:], 4)

    def join(mine, theirs):
        (joined,) = call(
            join_pieces, (1,), [(place_d, "smem", None)] + [full(a) for a in mine + theirs],
            [((width, mine[0].shape[1]), BF, None, None)],
            micros=3.0,
        )
        return joined

    def other_core(pieces):
        return tuple(swap_dp(piece, 1) for piece in pieces)

    def tokens_of(array, at):
        return lax.slice_in_dim(array, at * LENGTH, (at + 1) * LENGTH, axis=0)

    def sequence(array, at):
        return (array, (LENGTH, array.shape[1]), lambda *_: (at, 0))

    square = pltpu.VMEM((LENGTH, LENGTH), F32)
    heads = half // HD
    lanes = (LENGTH, half)
    masks = []
    for at in pair:
        seg, pad = tokens_of(segment_ids, at), tokens_of(pad_flags, at)
        masks.append([full(seg.reshape(-1, 1)), full(row(seg)), full(pad.reshape(-1, 1))])
    own_qkv = [full(w_query), full(w_key), full(w_value)]

    def attend(at, token):
        return call(
            attend_forward, (1,),
            [sequence(token, at)] + own_qkv + [full(row(b_query)), full(row(b_value)), full(row(b_up))]
            + masks[at],
            [(lanes, BF, None, None)] * 4
            + [((LENGTH + 8 * (at == 0), half), F32, None, None), ((heads, LENGTH), F32, None, None)],
            [square], micros=9.0,
        )

    shard = width // dp
    (proj,) = lock(swap_mp(eighth_t(w_proj)))
    down_y = swap_mp(lax.dynamic_slice_in_dim(w_down, d * shard, shard, 1).T.astype(F32))
    saved = [attend(0, lock(inputs, proj)[0])]
    proj, proj_near, up, down_y, saved[0] = lock(
        proj, near_pieces(proj), swap_mp(lock(eighth(w_up), proj)[0]), down_y, tuple(saved[0])
    )
    down_oth = lax.all_gather(down_y, "dp", axis=0, tiled=True)
    saved.append(attend(1, lock(inputs, proj)[0]))
    proj = (proj,) + tuple(proj_near)
    proj_far = far_pieces(*proj_near)
    ctx_a, up_near, proj_far, proj_core, saved[1] = lock(
        swap_mp(saved[0][4]), near_pieces(up), proj_far, other_core(proj), tuple(saved[1])
    )
    proj_far, proj_far_core, proj, proj_core = lock(
        proj_far, other_core(proj_far), proj, proj_core
    )

    steps = units // UNIT_BLOCK
    unit_row = lambda array: (array, (1, UNIT_BLOCK), lambda i: (0, i))
    unit_col = lambda array: (array, (array.shape[0], UNIT_BLOCK), lambda i: (0, i))
    unit_block = lambda array: (array, (UNIT_BLOCK, width), lambda i: (i, 0))
    unit_all = lambda array, block: (array, (array.shape[0], block), lambda i: (0, i))
    column = lambda array: (array, (array.shape[0], half), lambda i: (0, i))
    token = lambda dtype: ((LENGTH, width), dtype, None, None)
    stat = ((8, width), F32, None, None)
    def rows_of(at, cols, dtype, block=None):
        if block is None:
            return ((tokens, cols), dtype, (LENGTH, cols), lambda *_: (at, 0))
        return ((tokens, cols), dtype, (LENGTH, block), lambda i: (at, i))

    proj_oth = join(proj + tuple(proj_far), proj_core + tuple(proj_far_core))

    def forward_own(at, context, before):
        outs = call(
            feed_own, (steps,),
            [sequence(inputs, at), full(saved[at][3]), full(context), full(w_proj), full(proj_oth),
             full(row(b_proj)), full(row(gain_attn)), full(row(shift_attn)), full(row(b_down)),
             unit_col(w_up), unit_row(row(b_up)), unit_block(w_down)]
            + [(array, "any", None) for array in before],
            [token(BF), token(F32), rows_of(at, width, F32), rows_of(at, units, BF, UNIT_BLOCK),
             rows_of(at, units, BF, UNIT_BLOCK)],
            micros=8.0, alias={12 + i: 2 + i for i in range(len(before))},
        )
        return outs[0], outs[1], outs[2:]

    def forward_other(at, normed, before):
        return call(
            feed_up, (units // half,),
            [full(normed), column(joined), (ctx_a, (8, half), lambda i: (LENGTH // 8, 0))]
            + [(array, "any", None) for array in before],
            [rows_of(at, units, BF, half)] * 2, micros=4.0,
            alias={3 + i: i for i in range(len(before))},
        )

    normed_a, partial_a, kept = forward_own(0, ctx_a, ())
    up = (up,) + tuple(up_near)
    ctx_b, up_far, up_core, normed_a, partial_a, kept = lock(
        swap_mp(saved[1][4]), far_pieces(*up_near), other_core(up), normed_a, partial_a, tuple(kept)
    )
    up, up_far, up_far_core, up_core, normed_a, ctx_b = lock(
        up, up_far, other_core(up_far), up_core, normed_a, ctx_b
    )
    joined = join(up + tuple(up_far), up_core + tuple(up_far_core))
    other = forward_other(0, normed_a, ())
    normed_b, partial_b, (hidden, act_own, slope_own) = forward_own(1, ctx_b, kept)
    act_oth, slope_oth = forward_other(1, normed_b, other)
    every = lambda dtype: ((tokens, width), dtype, None, None)
    outputs, d_summed, d_ffn, stats_ffn, down_oth = call(
        feed_down, (1,),
        [full(act_oth), full(partial_a), full(partial_b), full(down_oth), full(row(gain_ffn)),
         full(row(shift_ffn)), full(cotangent)],
        [every(BF), every(F32), every(BF), stat, ((width, units), BF, None, None)], micros=10.0,
    )

    split = dp == 16
    core_arg = jnp.reshape(core, (1,)).astype(jnp.int32)
    lead = (2, 2, 2, width // dp)
    turned = pltpu.VMEM((width, tokens), BF)

    def parted(cols, block, index, extra=0):
        if not split:
            out = ((width + extra, cols), F32, (width + extra, block), lambda i: (0, index(i)))
            return [out]
        shape = lead[:-1] + (lead[-1] + extra,)
        return [(shape + (cols,), F32, shape + (block,), lambda i: (0, 0, 0, 0, index(i)))] * 2

    def pairs(outs):
        return outs[:len(outs) // 2], outs[len(outs) // 2:]

    bits = {"x": (d // 2) % 2, "l": (d // 4) % 2, "u": d // 8}
    hops = {"x": 2, "l": 4, "u": 8}

    class Reduction:
        def __init__(self, parts, order, terms=None):
            self.order, self.parts, self.terms = list(order), parts, terms

        def step(self):
            if not split:
                return self.parts[0]
            if self.terms is None:
                got = swap_dp(self.parts[1], 1)
                self.terms = [self.parts[0], got]
                return got
            stage = self.order.pop(0)
            bit = bits[stage]
            send = sum(pick(term, 1 - bit, 0) for term in self.terms)
            got = swap_dp(send, hops[stage])
            self.terms = [pick(term, bit, 0) for term in self.terms] + [got]
            return got

        def result(self):
            if not split:
                return lax.psum_scatter(self.parts[0], "dp", scatter_dimension=0, tiled=True)
            while self.order:
                self.step()
            return sum(self.terms)

    (down_whole,) = call(
        gradient, (units // UNIT_BLOCK,), [full(d_ffn), unit_all(act_own, UNIT_BLOCK)],
        [((width, units), F32, (width, UNIT_BLOCK), lambda i: (0, i))], [turned], 6.0,
    )
    d_ffn, down_whole = lock(d_ffn, down_whole)
    down_part = lax.psum_scatter(down_whole, "dp", scatter_dimension=0, tiled=True)
    back = lambda array: (array, (array.shape[0], BACK_BLOCK), lambda i: (0, i))
    d_up, sums_up, d_hidden, d_attn, d_context, stats_attn = call(
        feed_backward, (units // BACK_BLOCK,),
        [full(d_ffn), back(slope_own), back(slope_oth),
         (w_down, (BACK_BLOCK, width), lambda i: (i, 0)), back(down_oth), back(w_up), back(joined),
         full(d_summed), full(hidden), full(row(gain_attn)), full(w_proj)],
        [((tokens, units), BF, (tokens, BACK_BLOCK), lambda i: (0, i)),
         ((8, units), F32, (8, BACK_BLOCK), lambda i: (0, i)), every(F32), every(BF),
         ((tokens, half), BF, None, None), stat],
        [pltpu.VMEM((tokens, width), F32)], micros=20.0,
    )

    def back_attend(at, grad, before, sizes):
        q, k, v, _, _, lse = saved[at]
        outs = call(
            functools.partial(attend_backward, len(sizes)), (1,),
            [full(q), full(k), full(v), full(lse), sequence(grad, at)] + masks[at] + own_qkv
            + [(array, "any", None) for array in before],
            [rows_of(at, 3 * half, BF), ((8, 3 * half), F32, None, None)]
            + [((size, width), F32, None, None) for size in sizes],
            [square], micros=9.0, alias={11: 0} if before else {},
        )
        return outs[0], outs[1], list(outs[2:])

    blocks = units // half
    up = call(
        functools.partial(gradient_up, lead[-1]), (blocks + 1,),
        [(core_arg, "smem", None), full(normed_a), full(normed_b),
         (d_up, (tokens, half), lambda i: (0, jnp.minimum(i, blocks - 1))), full(d_attn),
         full(saved[0][3]), full(saved[1][3])],
        parted(units // 2, half, lambda i: jnp.minimum(i, blocks // 2 - 1))
        + parted(units // 2 + half, half, lambda i: jnp.maximum(i - blocks // 2, 0)),
        [turned], 9.0,
    )
    up, d_context = lock(up, d_context)
    up = [Reduction(parts, order) for parts, order in zip(pairs(up), UP_ORDERS)]

    def advance(reductions, *values):
        for one in reductions:
            one.step()
        if not split:
            return lock(*values)
        terms, *values = lock([one.terms for one in reductions], *values)
        for one, changed in zip(reductions, terms):
            one.terms = list(changed)
        return values

    dqkv, sums_a, mine_a = back_attend(0, d_context, (), (256, 256))
    dqkv, mine_a, d_context = advance(up, dqkv, mine_a, d_context)
    theirs_a = [swap_mp(mine_a[0])]
    dqkv, sums_b, mine_b = back_attend(1, d_context, (dqkv,), (256, 128, 128))
    sums_rows = 6 + units // width
    last = call(
        functools.partial(gradient_attention, lead[-1]), (1,),
        [(core_arg, "smem", None), full(inputs), full(dqkv)]
        + [full(a) for a in (stats_ffn, stats_attn, sums_up, sums_a, sums_b)],
        parted(2 * half, 2 * half, lambda i: 0, sums_rows) + parted(half, half, lambda i: 0, 8),
        [turned], 7.0,
    )
    last, mine_a, mine_b, theirs_a = advance(up, last, mine_a, mine_b, theirs_a)
    query, value = [Reduction(parts, order) for parts, order in zip(pairs(last), LAST_ORDERS)]
    theirs_a.append(swap_mp(mine_a[1]))
    mine_b, theirs_a, down_part = advance(up + [query, value], mine_b, theirs_a, down_part)
    theirs_b = []
    for moving in (up + [query, value], [query, value]):
        theirs_b.append(swap_mp(mine_b[len(theirs_b)]))
        mine_b, theirs_b = advance(moving, mine_b, theirs_b)
    theirs_b.append(swap_mp(mine_b[2]))
    if split:
        query_part, value_part = query.result(), value.result()
        vectors, biases = query_part[shard:], value_part[shard:]
    else:
        (whole,), (value_whole,) = query.parts, value.parts
        vectors, biases = lax.psum((whole[width:], value_whole[width:]), "dp")
        query_part, value_part = (
            lax.psum_scatter(one[:width], "dp", scatter_dimension=0, tiled=True)
            for one in (whole, value_whole)
        )
    value_part = value_part[:shard]
    query_part = query_part[:shard]
    up_part = [one.result() for one in up]
    proj_part = up_part[1][:, units // 2:]
    up_part = jnp.concatenate([up_part[0], up_part[1][:, :units // 2]], axis=1)

    grad_inputs = None
    for at, (mine, theirs) in enumerate(((mine_a, theirs_a), (mine_b, theirs_b))):
        ins = [sequence(d_hidden, at)] + [full(a) for a in list(mine) + list(theirs)]
        before = len(ins)
        if grad_inputs is not None:
            ins.append((grad_inputs, "any", None))
        (grad_inputs,) = call(
            functools.partial(input_total, len(mine)), (1,), ins, [rows_of(at, width, F32)],
            micros=2.5, alias={} if at == 0 else {before: 0},
        )
    return (
        outputs,
        grad_inputs,
        query_part[:, :half],
        query_part[:, half:],
        value_part,
        biases[0],
        biases[1],
        proj_part.T,
        vectors[5],
        vectors[3],
        vectors[4],
        up_part,
        vectors[6:8].reshape(-1),
        down_part.T,
        vectors[2],
        vectors[0],
        vectors[1],
    )


def solution(mesh):
    placed = (
        P("dp", None), P("dp"), P("dp"), P(None, "mp"), P(None, "mp"), P(None, "mp"), P("mp"),
        P("mp"), P("mp", None), P(), P(), P(), P(None, "mp"), P("mp"), P("mp", None), P(), P(), P(),
        P("dp", None),
    )
    return jax.shard_map(
        functools.partial(on_device, mesh.shape["dp"]),
        mesh=mesh,
        in_specs=placed,
        out_specs=(
            P("dp", None), P("dp", None), P("dp", "mp"), P("dp", "mp"), P("dp", "mp"), P("mp"),
            P("mp"), P("mp", "dp"), P(), P(), P(), P("dp", "mp"), P("mp"), P("mp", "dp"), P(), P(),
            P(),
        ),
        check_vma=False,
    )
```

```python
import functools
import math

import jax
import jax.numpy as jnp
from jax import lax
from jax.experimental import pallas as pl
from jax.experimental.pallas import tpu as pltpu
from jax.sharding import PartitionSpec as P

HD = 64
LENGTH = 512
QUERY_CHUNK = 256
UNIT_BLOCK = 512
BACK_BLOCK = 256
UP_ORDERS = ("lux", "xlu")
LAST_ORDERS = ("xlu", "lux")
norm_eps = 1e-05
masked_value = -1000000000.0
BF = jnp.bfloat16
F32 = jnp.float32
VMEM_BYTES = 50 * 1024 * 1024


def nn(a, b):
    return lax.dot_general(a, b, (((1,), (0,)), ((), ())), preferred_element_type=F32)


def nt(a, b):
    return lax.dot_general(a, b, (((1,), (1,)), ((), ())), preferred_element_type=F32)


def call(body, grid, ins, outs, scratch=(), micros=1.0, alias=None):
    def spec(shape, block, index):
        if block == "smem":
            return pl.BlockSpec(memory_space=pltpu.SMEM)
        if block == "any":
            return pl.BlockSpec(memory_space=pl.ANY)
        if block is None:
            return pl.BlockSpec(shape, lambda *_: (0,) * len(shape))
        return pl.BlockSpec(block, index)

    moved = sum(a.size * a.dtype.itemsize for a, _, _ in ins)
    moved += sum(math.prod(s) * jnp.dtype(d).itemsize for s, d, _, _ in outs)
    return pl.pallas_call(
        body,
        grid=grid,
        in_specs=[spec(a.shape, b, i) for a, b, i in ins],
        out_specs=[spec(s, b, i) for s, _, b, i in outs],
        out_shape=[jax.ShapeDtypeStruct(s, d) for s, d, _, _ in outs],
        scratch_shapes=list(scratch),
        input_output_aliases=alias or {},
        compiler_params=pltpu.CompilerParams(vmem_limit_bytes=VMEM_BYTES),
        cost_estimate=pl.CostEstimate(
            flops=int(micros * 1.15e9), bytes_accessed=moved, transcendentals=0
        ),
    )(*[a for a, _, _ in ins])


def mask_bias(segc_ref, segr_ref, padc_ref, bias_ref):
    shape = bias_ref.shape
    key = lax.broadcasted_iota(jnp.int32, shape, 0)
    query = lax.broadcasted_iota(jnp.int32, shape, 1)
    same = segc_ref[...] == segr_ref[...]
    allowed = same & ((padc_ref[...] == 0) | (key == query))
    bias_ref[...] = jnp.where(allowed, 0.0, masked_value)


def attend_forward(
    x_ref, wq_ref, wk_ref, wv_ref, bq_ref, bv_ref, bu_ref, segc_ref, segr_ref, padc_ref,
    q_ref, k_ref, v_ref, ctx_ref, send_ref, lse_ref, bias_ref,
):
    x = x_ref[...]
    q_ref[...] = ((nn(x, wq_ref[...]) + bq_ref[...]).astype(BF).astype(F32) * HD ** (-0.5)).astype(BF)
    k_ref[...] = nn(x, wk_ref[...]).astype(BF)
    v_ref[...] = (nn(x, wv_ref[...]) + bv_ref[...]).astype(BF)
    mask_bias(segc_ref, segr_ref, padc_ref, bias_ref)
    length, wide = x.shape[0], q_ref.shape[1]
    if send_ref.shape[0] > length:
        send_ref[length:] = jnp.zeros((send_ref.shape[0] - length, wide), F32)
        for at in range(bu_ref.shape[1] // wide):
            send_ref[length + at:length + at + 1] = bu_ref[:, at * wide:(at + 1) * wide]

    def pair(index, carry):
        cols = pl.ds(pl.multiple_of(index * 128, 128), 128)
        keys = k_ref[:, cols]
        values_t = v_ref[:, cols].T
        lane = lax.broadcasted_iota(jnp.int32, (QUERY_CHUNK, 128), 1)
        for start in range(0, length, QUERY_CHUNK):
            rows = pl.ds(start, QUERY_CHUNK)
            query = q_ref[rows, cols]
            parts = []
            for head in range(2):
                one = jnp.where((lane < HD) == (head == 0), query, jnp.zeros_like(query))
                scores = nt(keys, one) + bias_ref[:, rows]
                highest = jnp.max(scores, axis=0, keepdims=True)
                grown = jnp.exp(scores - highest)
                total = jnp.sum(grown, axis=0, keepdims=True)
                weights = (grown * (1.0 / total)).astype(BF)
                lse_ref[pl.ds(2 * index + head, 1), rows] = highest + jnp.log(total)
                parts.append(nn(values_t[head * HD:(head + 1) * HD], weights))
            context = jnp.concatenate(parts, axis=0).T.astype(BF)
            ctx_ref[rows, cols] = context
            send_ref[rows, cols] = context.astype(F32)
        return carry

    lax.fori_loop(0, q_ref.shape[1] // 128, pair, 0)


def attend_backward(
    parts, q_ref, k_ref, v_ref, lse_ref, dctx_ref, segc_ref, segr_ref, padc_ref, wq_ref, wk_ref, wv_ref, *rest
):
    bias_ref, part_refs = rest[-1], rest[-1 - parts:-1]
    dqkv_ref, sums_ref = rest[-3 - parts:-1 - parts]
    mask_bias(segc_ref, segr_ref, padc_ref, bias_ref)
    length, width = q_ref.shape

    def pair(index, carry):
        first = pl.multiple_of(index * 128, 128)
        cols = pl.ds(first, 128)
        keys = k_ref[:, cols]
        values = v_ref[:, cols]
        keys_t = keys.T
        lane = lax.broadcasted_iota(jnp.int32, (QUERY_CHUNK, 128), 1)
        d_keys = [None, None]
        d_values = [None, None]
        for start in range(0, length, QUERY_CHUNK):
            rows = pl.ds(start, QUERY_CHUNK)
            query = q_ref[rows, cols]
            grad = dctx_ref[rows, cols]
            d_query = []
            for head in range(2):
                here = (lane < HD) == (head == 0)
                scores = nt(keys, jnp.where(here, query, jnp.zeros_like(query))) + bias_ref[:, rows]
                prob = jnp.exp(scores - lse_ref[pl.ds(2 * index + head, 1), rows])
                weights = prob.astype(BF)
                d_prob = nt(values, jnp.where(here, grad, jnp.zeros_like(grad)))
                inner = jnp.sum(prob * d_prob, axis=0, keepdims=True)
                raw = (prob * (d_prob - inner)).astype(BF)
                dv = nn(weights, grad)
                dk = nn(raw, query)
                d_values[head] = dv if start == 0 else d_values[head] + dv
                d_keys[head] = dk if start == 0 else d_keys[head] + dk
                d_query.append(nn(keys_t[head * HD:(head + 1) * HD], raw))
            dq = (jnp.concatenate(d_query, axis=0).T * HD ** (-0.5)).astype(BF)
            dqkv_ref[rows, cols] = dq
        full = lax.broadcasted_iota(jnp.int32, (length, 128), 1) < HD
        dqkv_ref[:, pl.ds(pl.multiple_of(width + first, 128), 128)] = jnp.where(
            full, d_keys[0], d_keys[1]
        ).astype(BF)
        dqkv_ref[:, pl.ds(pl.multiple_of(2 * width + first, 128), 128)] = jnp.where(
            full, d_values[0], d_values[1]
        ).astype(BF)
        return carry

    lax.fori_loop(0, width // 128, pair, 0)
    sums_ref[...] = jnp.broadcast_to(
        jnp.sum(dqkv_ref[...].astype(F32), axis=0, keepdims=True), sums_ref.shape
    )
    total = None
    for part, weight in enumerate((wq_ref, wk_ref, wv_ref)):
        term = nt(dqkv_ref[:, part * width:(part + 1) * width], weight[...])
        total = term if total is None else total + term
    at = 0
    for part_ref in part_refs:
        part_ref[...] = total[at:at + part_ref.shape[0]]
        at += part_ref.shape[0]


def moments(values):
    average = jnp.mean(values, axis=-1, keepdims=True)
    centered = values - average
    variance = jnp.mean(centered * centered, axis=-1, keepdims=True)
    inverse = lax.rsqrt(variance + norm_eps)
    return centered * inverse, inverse


def norm_backward(upstream, n, inverse, gain):
    scaled = upstream * gain
    return inverse * (
        scaled
        - jnp.mean(scaled, axis=-1, keepdims=True)
        - n * jnp.mean(scaled * n, axis=-1, keepdims=True)
    )


def down_sum(values):
    return jnp.sum(values, axis=0, keepdims=True)


def activate(nlow, wu_ref, bias, act_ref, slope_ref):
    up = nn(nlow, wu_ref[...]) + bias
    cdf = 0.5 * (1.0 + lax.erf(up * 2.0 ** (-0.5)))
    active = (up * cdf).astype(BF)
    act_ref[...] = active
    slope = cdf + up * jnp.exp(-0.5 * up * up) * (1.0 / math.sqrt(2.0 * math.pi))
    slope_ref[...] = slope.astype(BF)
    return active


def feed_own(
    x_ref, co_ref, cx_ref, wpo_ref, wpx_ref, bp_ref, g_ref, s_ref, bd_ref, wu_ref, bu_ref, wd_ref, *rest
):
    nlow_ref, acc_ref, hid_ref, act_ref, slope_ref = rest[-5:]

    @pl.when(pl.program_id(0) == 0)
    def _():
        attn = nn(co_ref[...], wpo_ref[...]) + nt(cx_ref[:x_ref.shape[0]].astype(BF), wpx_ref[...]) + bp_ref[...]
        hidden = x_ref[...].astype(F32) + attn
        hid_ref[...] = hidden
        n, _ = moments(hidden)
        normed = n * g_ref[...] + s_ref[...]
        nlow_ref[...] = normed.astype(BF)
        acc_ref[...] = normed + bd_ref[...]

    acc_ref[...] += nn(activate(nlow_ref[...], wu_ref, bu_ref[...], act_ref, slope_ref), wd_ref[...])


def feed_up(nlow_ref, wu_ref, bu_ref, *rest):
    bias = bu_ref[pl.ds(pl.program_id(0), 1), :]
    activate(nlow_ref[...], wu_ref, bias, *rest[-2:])


def feed_down(
    act_ref, starta_ref, startb_ref, wd_ref, g_ref, s_ref, cot_ref,
    out_ref, dsum_ref, dffn_ref, stats_ref, low_ref,
):
    weights = wd_ref[...].astype(BF)
    low_ref[...] = weights
    stats_ref[...] = jnp.zeros_like(stats_ref)
    length = starta_ref.shape[0]
    for at, start_ref in enumerate((starta_ref, startb_ref)):
        rows = pl.ds(at * length, length)
        total = start_ref[...] + nt(act_ref[rows, :], weights)
        n, inverse = moments(total)
        out_ref[rows, :] = (n * g_ref[...] + s_ref[...]).astype(BF)
        cot = cot_ref[rows, :].astype(F32)
        d_summed = norm_backward(cot, n, inverse, g_ref[...])
        d_ffn = d_summed.astype(BF)
        dsum_ref[rows, :] = d_summed
        dffn_ref[rows, :] = d_ffn
        stats_ref[0:1] += down_sum(cot * n)
        stats_ref[1:2] += down_sum(cot)
        stats_ref[2:3] += down_sum(d_ffn.astype(F32))


def feed_backward(
    dffn_ref, so_ref, sx_ref, wdo_ref, wdx_ref, wuo_ref, wux_ref, dsum_ref, hid_ref, g_ref, wpo_ref,
    duo_ref, bup_ref, dhid_ref, dattn_ref, dctx_ref, stats_ref, acc_ref,
):
    @pl.when(pl.program_id(0) == 0)
    def _():
        acc_ref[...] = dsum_ref[...]

    d_ffn = dffn_ref[...]
    d_own = (nt(d_ffn, wdo_ref[...]) * so_ref[...].astype(F32)).astype(BF)
    d_other = (nn(d_ffn, wdx_ref[...]) * sx_ref[...].astype(F32)).astype(BF)
    duo_ref[...] = d_own
    bup_ref[...] = jnp.broadcast_to(down_sum(d_own.astype(F32)), bup_ref.shape)
    acc_ref[...] += nt(d_own, wuo_ref[...]) + nt(d_other, wux_ref[...])

    @pl.when(pl.program_id(0) == pl.num_programs(0) - 1)
    def _():
        d_normed = acc_ref[...]
        n, inverse = moments(hid_ref[...])
        d_hidden = norm_backward(d_normed, n, inverse, g_ref[...])
        d_attn = d_hidden.astype(BF)
        dhid_ref[...] = d_hidden
        dattn_ref[...] = d_attn
        dctx_ref[...] = nt(d_attn, wpo_ref[...]).astype(BF)
        stats_ref[...] = jnp.zeros_like(stats_ref)
        stats_ref[0:1] = down_sum(d_normed * n)
        stats_ref[1:2] = down_sum(d_normed)
        stats_ref[2:3] = down_sum(d_attn.astype(F32))


def input_total(parts, dhid_ref, *refs):
    at = 0
    for mine_ref, theirs_ref in zip(refs[:parts], refs[parts:2 * parts]):
        rows = pl.ds(at, mine_ref.shape[0])
        refs[-1][rows, :] = dhid_ref[rows, :] + (mine_ref[...] + theirs_ref[...])
        at += mine_ref.shape[0]


def put(g, core_ref, outs, rows, order, extra=None):
    if len(outs) == 1:
        outs[0][:g.shape[0]] = g
        if extra is not None:
            outs[0][g.shape[0]:] = extra
        return
    keep_ref, send_ref = outs
    first = core_ref[0] == 0
    for block in range(8):
        at = 2 * block * rows
        even, odd = g[at:at + rows], g[at + rows:at + 2 * rows]
        bits = {"u": block // 4, "l": block // 2 % 2, "x": block % 2}
        place = tuple(bits[stage] for stage in order)
        keep_ref[place + (slice(0, rows),)] = jnp.where(first, even, odd)
        send_ref[place + (slice(0, rows),)] = jnp.where(first, odd, even)
        if extra is not None:
            keep_ref[place + (slice(rows, None),)] = extra
            send_ref[place + (slice(rows, None),)] = extra


def turn(refs, turned, step=0):
    @pl.when(pl.program_id(0) == step)
    def _():
        at = 0
        for ref in refs:
            turned[:, at:at + ref.shape[0]] = ref[...].T
            at += ref.shape[0]


def gradient(left_ref, right_ref, out_ref, turned):
    turn((left_ref,), turned)
    out_ref[...] = nn(turned[...], right_ref[...])


def gradient_up(rows, core_ref, la_ref, lb_ref, right_ref, proj_ref, ca_ref, cb_ref, *rest):
    turned, outs = rest[-1], rest[:-1]
    last = pl.num_programs(0) - 1
    count = len(outs) // 2
    length = la_ref.shape[0]
    turn((la_ref, lb_ref), turned)
    turn((proj_ref,), turned, last)

    @pl.when(pl.program_id(0) < last // 2)
    def _():
        put(nn(turned[...], right_ref[...]), core_ref, outs[:count], rows, UP_ORDERS[0])

    @pl.when((pl.program_id(0) >= last // 2) & (pl.program_id(0) < last))
    def _():
        put(nn(turned[...], right_ref[...]), core_ref, outs[count:], rows, UP_ORDERS[1])

    @pl.when(pl.program_id(0) == last)
    def _():
        g = nn(turned[:, :length], ca_ref[...]) + nn(turned[:, length:], cb_ref[...])
        put(g, core_ref, outs[count:], rows, UP_ORDERS[1])


def gradient_attention(
    rows, core_ref, x_ref, dqkv_ref, f_ref, a_ref, up_ref, ka_ref, kb_ref, *rest
):
    turned, outs = rest[-1], rest[:-1]
    count = len(outs) // 2
    width = x_ref.shape[1]
    half = width // 2
    up, qkv = up_ref[...], ka_ref[...] + kb_ref[...]
    pieces = [f_ref[:3], a_ref[:3]] + [
        up[:1, at * width:(at + 1) * width] for at in range(up.shape[1] // width)
    ]
    extra = jnp.concatenate(pieces, axis=0)
    biases = jnp.concatenate([qkv[:1, :half], qkv[:1, 2 * half:], jnp.zeros((6, half), F32)], axis=0)
    turn((x_ref,), turned)
    put(nn(turned[...], dqkv_ref[:, :2 * half]), core_ref, outs[:count], rows, LAST_ORDERS[0], extra)
    put(nn(turned[...], dqkv_ref[:, 2 * half:]), core_ref, outs[count:], rows, LAST_ORDERS[1], biases)


def join_pieces(place_ref, *refs):
    out_ref = refs[-1]
    rows = refs[0].shape[0]
    for mine in (True, False):
        base = (place_ref[0] if mine else 1 - place_ref[0]) * 4
        pieces = refs[:5] if mine else refs[5:10]
        starts = [base + jnp.bitwise_xor(place_ref[1], piece) for piece in (0, 1, 2, 3, 3)]
        for index, (at, piece) in enumerate(zip(starts, pieces)):
            start = at * rows + (rows // 2 if index == 4 else 0)
            out_ref[pl.ds(pl.multiple_of(start, 16), piece.shape[0])] = piece[...].astype(BF)


def pick(array, index, axis):
    return lax.dynamic_index_in_dim(array, index, axis, keepdims=False)


def lock(*values):
    return lax.optimization_barrier(values)


def on_device(
    dp, inputs, segment_ids, pad_flags, w_query, w_key, w_value, b_query, b_value, w_proj, b_proj,
    gain_attn, shift_attn, w_up, b_up, w_down, b_down, gain_ffn, shift_ffn, cotangent,
):
    d = lax.axis_index("dp")
    tokens, width = inputs.shape
    half = w_query.shape[1]
    units = w_up.shape[1]
    core, low = d % 2, (d // 2) % 4
    pair = range(tokens // LENGTH)

    def swap_mp(array):
        return lax.ppermute(array, "mp", [(0, 1), (1, 0)])

    def swap_dp(array, bit):
        return lax.ppermute(array, "dp", [(i, i ^ bit) for i in range(dp)])

    def row(vector):
        return vector.reshape(1, -1)

    full = lambda array: (array, None, None)

    rows = width // 8
    place_d = jnp.stack([core, low]).astype(jnp.int32)

    def eighth(weight):
        return lax.dynamic_slice_in_dim(weight, (core * 4 + low) * rows, rows, 0).astype(F32)

    def eighth_t(weight):
        return lax.dynamic_slice_in_dim(weight, (core * 4 + low) * rows, rows, 1).T.astype(F32)

    def near_pieces(own):
        return swap_dp(own, 2), swap_dp(own, 4)

    def far_pieces(by_x, by_z):
        return swap_dp(by_z[:rows // 2], 2), swap_dp(by_x[rows // 2:], 4)

    def join(mine, theirs):
        (joined,) = call(
            join_pieces, (1,), [(place_d, "smem", None)] + [full(a) for a in mine + theirs],
            [((width, mine[0].shape[1]), BF, None, None)],
            micros=3.0,
        )
        return joined

    def other_core(pieces):
        return tuple(swap_dp(piece, 1) for piece in pieces)

    def tokens_of(array, at):
        return lax.slice_in_dim(array, at * LENGTH, (at + 1) * LENGTH, axis=0)

    def sequence(array, at):
        return (array, (LENGTH, array.shape[1]), lambda *_: (at, 0))

    square = pltpu.VMEM((LENGTH, LENGTH), F32)
    heads = half // HD
    lanes = (LENGTH, half)
    masks = []
    for at in pair:
        seg, pad = tokens_of(segment_ids, at), tokens_of(pad_flags, at)
        masks.append([full(seg.reshape(-1, 1)), full(row(seg)), full(pad.reshape(-1, 1))])
    own_qkv = [full(w_query), full(w_key), full(w_value)]

    def attend(at, token):
        return call(
            attend_forward, (1,),
            [sequence(token, at)] + own_qkv + [full(row(b_query)), full(row(b_value)), full(row(b_up))]
            + masks[at],
            [(lanes, BF, None, None)] * 4
            + [((LENGTH + 8 * (at == 0), half), F32, None, None), ((heads, LENGTH), F32, None, None)],
            [square], micros=9.0,
        )

    shard = width // dp
    (proj,) = lock(swap_mp(eighth_t(w_proj)))
    down_y = swap_mp(lax.dynamic_slice_in_dim(w_down, d * shard, shard, 1).T.astype(F32))
    saved = [attend(0, lock(inputs, proj)[0])]
    proj, proj_near, up, down_y, saved[0] = lock(
        proj, near_pieces(proj), swap_mp(eighth(w_up)), down_y, tuple(saved[0])
    )
    down_oth = lax.all_gather(down_y, "dp", axis=0, tiled=True)
    saved.append(attend(1, lock(inputs, proj)[0]))
    proj = (proj,) + tuple(proj_near)
    proj_far = far_pieces(*proj_near)
    ctx_a, up_near, proj_far, proj_core, saved[1] = lock(
        swap_mp(saved[0][4]), near_pieces(up), proj_far, other_core(proj), tuple(saved[1])
    )
    proj_far, proj_far_core, proj, proj_core = lock(
        proj_far, other_core(proj_far), proj, proj_core
    )

    steps = units // UNIT_BLOCK
    unit_row = lambda array: (array, (1, UNIT_BLOCK), lambda i: (0, i))
    unit_col = lambda array: (array, (array.shape[0], UNIT_BLOCK), lambda i: (0, i))
    unit_block = lambda array: (array, (UNIT_BLOCK, width), lambda i: (i, 0))
    unit_all = lambda array, block: (array, (array.shape[0], block), lambda i: (0, i))
    column = lambda array: (array, (array.shape[0], half), lambda i: (0, i))
    token = lambda dtype: ((LENGTH, width), dtype, None, None)
    stat = ((8, width), F32, None, None)
    def rows_of(at, cols, dtype, block=None):
        if block is None:
            return ((tokens, cols), dtype, (LENGTH, cols), lambda *_: (at, 0))
        return ((tokens, cols), dtype, (LENGTH, block), lambda i: (at, i))

    proj_oth = join(proj + tuple(proj_far), proj_core + tuple(proj_far_core))

    def forward_own(at, context, before):
        outs = call(
            feed_own, (steps,),
            [sequence(inputs, at), full(saved[at][3]), full(context), full(w_proj), full(proj_oth),
             full(row(b_proj)), full(row(gain_attn)), full(row(shift_attn)), full(row(b_down)),
             unit_col(w_up), unit_row(row(b_up)), unit_block(w_down)]
            + [(array, "any", None) for array in before],
            [token(BF), token(F32), rows_of(at, width, F32), rows_of(at, units, BF, UNIT_BLOCK),
             rows_of(at, units, BF, UNIT_BLOCK)],
            micros=8.0, alias={12 + i: 2 + i for i in range(len(before))},
        )
        return outs[0], outs[1], outs[2:]

    def forward_other(at, normed, before):
        return call(
            feed_up, (units // half,),
            [full(normed), column(joined), (ctx_a, (8, half), lambda i: (LENGTH // 8, 0))]
            + [(array, "any", None) for array in before],
            [rows_of(at, units, BF, half)] * 2, micros=4.0,
            alias={3 + i: i for i in range(len(before))},
        )

    normed_a, partial_a, kept = forward_own(0, ctx_a, ())
    up = (up,) + tuple(up_near)
    ctx_b, up_far, up_core, normed_a, partial_a, kept = lock(
        swap_mp(saved[1][4]), far_pieces(*up_near), other_core(up), normed_a, partial_a, tuple(kept)
    )
    up, up_far, up_far_core, up_core, normed_a, ctx_b = lock(
        up, up_far, other_core(up_far), up_core, normed_a, ctx_b
    )
    joined = join(up + tuple(up_far), up_core + tuple(up_far_core))
    other = forward_other(0, normed_a, ())
    normed_b, partial_b, (hidden, act_own, slope_own) = forward_own(1, ctx_b, kept)
    act_oth, slope_oth = forward_other(1, normed_b, other)
    every = lambda dtype: ((tokens, width), dtype, None, None)
    outputs, d_summed, d_ffn, stats_ffn, down_oth = call(
        feed_down, (1,),
        [full(act_oth), full(partial_a), full(partial_b), full(down_oth), full(row(gain_ffn)),
         full(row(shift_ffn)), full(cotangent)],
        [every(BF), every(F32), every(BF), stat, ((width, units), BF, None, None)], micros=10.0,
    )

    split = dp == 16
    core_arg = jnp.reshape(core, (1,)).astype(jnp.int32)
    lead = (2, 2, 2, width // dp)
    turned = pltpu.VMEM((width, tokens), BF)

    def parted(cols, block, index, extra=0):
        if not split:
            out = ((width + extra, cols), F32, (width + extra, block), lambda i: (0, index(i)))
            return [out]
        shape = lead[:-1] + (lead[-1] + extra,)
        return [(shape + (cols,), F32, shape + (block,), lambda i: (0, 0, 0, 0, index(i)))] * 2

    def pairs(outs):
        return outs[:len(outs) // 2], outs[len(outs) // 2:]

    bits = {"x": (d // 2) % 2, "l": (d // 4) % 2, "u": d // 8}
    hops = {"x": 2, "l": 4, "u": 8}

    class Reduction:
        def __init__(self, parts, order, terms=None):
            self.order, self.parts, self.terms = list(order), parts, terms

        def step(self):
            if not split:
                return self.parts[0]
            if self.terms is None:
                got = swap_dp(self.parts[1], 1)
                self.terms = [self.parts[0], got]
                return got
            stage = self.order.pop(0)
            bit = bits[stage]
            send = sum(pick(term, 1 - bit, 0) for term in self.terms)
            got = swap_dp(send, hops[stage])
            self.terms = [pick(term, bit, 0) for term in self.terms] + [got]
            return got

        def result(self):
            if not split:
                return lax.psum_scatter(self.parts[0], "dp", scatter_dimension=0, tiled=True)
            while self.order:
                self.step()
            return sum(self.terms)

    (down_whole,) = call(
        gradient, (units // UNIT_BLOCK,), [full(d_ffn), unit_all(act_own, UNIT_BLOCK)],
        [((width, units), F32, (width, UNIT_BLOCK), lambda i: (0, i))], [turned], 6.0,
    )
    d_ffn, down_whole = lock(d_ffn, down_whole)
    down_part = lax.psum_scatter(down_whole, "dp", scatter_dimension=0, tiled=True)
    back = lambda array: (array, (array.shape[0], BACK_BLOCK), lambda i: (0, i))
    d_up, sums_up, d_hidden, d_attn, d_context, stats_attn = call(
        feed_backward, (units // BACK_BLOCK,),
        [full(d_ffn), back(slope_own), back(slope_oth),
         (w_down, (BACK_BLOCK, width), lambda i: (i, 0)), back(down_oth), back(w_up), back(joined),
         full(d_summed), full(hidden), full(row(gain_attn)), full(w_proj)],
        [((tokens, units), BF, (tokens, BACK_BLOCK), lambda i: (0, i)),
         ((8, units), F32, (8, BACK_BLOCK), lambda i: (0, i)), every(F32), every(BF),
         ((tokens, half), BF, None, None), stat],
        [pltpu.VMEM((tokens, width), F32)], micros=20.0,
    )

    def back_attend(at, grad, before, sizes):
        q, k, v, _, _, lse = saved[at]
        outs = call(
            functools.partial(attend_backward, len(sizes)), (1,),
            [full(q), full(k), full(v), full(lse), sequence(grad, at)] + masks[at] + own_qkv
            + [(array, "any", None) for array in before],
            [rows_of(at, 3 * half, BF), ((8, 3 * half), F32, None, None)]
            + [((size, width), F32, None, None) for size in sizes],
            [square], micros=9.0, alias={11: 0} if before else {},
        )
        return outs[0], outs[1], list(outs[2:])

    blocks = units // half
    up = call(
        functools.partial(gradient_up, lead[-1]), (blocks + 1,),
        [(core_arg, "smem", None), full(normed_a), full(normed_b),
         (d_up, (tokens, half), lambda i: (0, jnp.minimum(i, blocks - 1))), full(d_attn),
         full(saved[0][3]), full(saved[1][3])],
        parted(units // 2, half, lambda i: jnp.minimum(i, blocks // 2 - 1))
        + parted(units // 2 + half, half, lambda i: jnp.maximum(i - blocks // 2, 0)),
        [turned], 9.0,
    )
    up, d_context = lock(up, d_context)
    up = [Reduction(parts, order) for parts, order in zip(pairs(up), UP_ORDERS)]

    def advance(reductions, *values):
        for one in reductions:
            one.step()
        if not split:
            return lock(*values)
        terms, *values = lock([one.terms for one in reductions], *values)
        for one, changed in zip(reductions, terms):
            one.terms = list(changed)
        return values

    dqkv, sums_a, mine_a = back_attend(0, d_context, (), (256, 256))
    dqkv, mine_a, d_context = advance(up, dqkv, mine_a, d_context)
    theirs_a = [swap_mp(mine_a[0])]
    dqkv, sums_b, mine_b = back_attend(1, d_context, (dqkv,), (256, 128, 128))
    sums_rows = 6 + units // width
    last = call(
        functools.partial(gradient_attention, lead[-1]), (1,),
        [(core_arg, "smem", None), full(inputs), full(dqkv)]
        + [full(a) for a in (stats_ffn, stats_attn, sums_up, sums_a, sums_b)],
        parted(2 * half, 2 * half, lambda i: 0, sums_rows) + parted(half, half, lambda i: 0, 8),
        [turned], 7.0,
    )
    last, mine_a, mine_b, theirs_a = advance(up, last, mine_a, mine_b, theirs_a)
    query, value = [Reduction(parts, order) for parts, order in zip(pairs(last), LAST_ORDERS)]
    theirs_a.append(swap_mp(mine_a[1]))
    mine_b, theirs_a, down_part = advance(up + [query, value], mine_b, theirs_a, down_part)
    theirs_b = []
    for moving in (up + [query, value], [query, value]):
        theirs_b.append(swap_mp(mine_b[len(theirs_b)]))
        mine_b, theirs_b = advance(moving, mine_b, theirs_b)
    theirs_b.append(swap_mp(mine_b[2]))
    if split:
        query_part, value_part = query.result(), value.result()
        vectors, biases = query_part[shard:], value_part[shard:]
    else:
        (whole,), (value_whole,) = query.parts, value.parts
        vectors, biases = lax.psum((whole[width:], value_whole[width:]), "dp")
        query_part, value_part = (
            lax.psum_scatter(one[:width], "dp", scatter_dimension=0, tiled=True)
            for one in (whole, value_whole)
        )
    value_part = value_part[:shard]
    query_part = query_part[:shard]
    up_part = [one.result() for one in up]
    proj_part = up_part[1][:, units // 2:]
    up_part = jnp.concatenate([up_part[0], up_part[1][:, :units // 2]], axis=1)

    grad_inputs = None
    for at, (mine, theirs) in enumerate(((mine_a, theirs_a), (mine_b, theirs_b))):
        ins = [sequence(d_hidden, at)] + [full(a) for a in list(mine) + list(theirs)]
        before = len(ins)
        if grad_inputs is not None:
            ins.append((grad_inputs, "any", None))
        (grad_inputs,) = call(
            functools.partial(input_total, len(mine)), (1,), ins, [rows_of(at, width, F32)],
            micros=2.5, alias={} if at == 0 else {before: 0},
        )
    return (
        outputs,
        grad_inputs,
        query_part[:, :half],
        query_part[:, half:],
        value_part,
        biases[0],
        biases[1],
        proj_part.T,
        vectors[5],
        vectors[3],
        vectors[4],
        up_part,
        vectors[6:8].reshape(-1),
        down_part.T,
        vectors[2],
        vectors[0],
        vectors[1],
    )


def solution(mesh):
    placed = (
        P("dp", None), P("dp"), P("dp"), P(None, "mp"), P(None, "mp"), P(None, "mp"), P("mp"),
        P("mp"), P("mp", None), P(), P(), P(), P(None, "mp"), P("mp"), P("mp", None), P(), P(), P(),
        P("dp", None),
    )
    return jax.shard_map(
        functools.partial(on_device, mesh.shape["dp"]),
        mesh=mesh,
        in_specs=placed,
        out_specs=(
            P("dp", None), P("dp", None), P("dp", "mp"), P("dp", "mp"), P("dp", "mp"), P("mp"),
            P("mp"), P("mp", "dp"), P(), P(), P(), P("dp", "mp"), P("mp"), P("mp", "dp"), P(), P(),
            P(),
        ),
        check_vma=False,
    )
```
